32 devices in a mesh: dp: 4 (over z), tm: 4 (over y, x), tile: 2 (over core).
Axes of the slice: x: 2, y: 2, z: 4, core: 2. Of those that a mesh axis runs over, the one named last changes fastest.
Arguments:
- activations: bfloat16 [4, 32, 16, 32, 128], P('dp', 'tm', 'tile'), may hold values from -6 to 6
- kernel: bfloat16 [3456, 128], replicated, may hold values from -0.109375 to 0.109375
- conv_bias: float32 [128], replicated, may hold values from -3 to 3
- cotangent: bfloat16 [4, 32, 16, 32, 128], P('dp', 'tm', 'tile'), may hold values from -6 to 6
Outputs:
- block_out: bfloat16 [4, 32, 16, 32, 128], P('dp', 'tm', 'tile')
- grad_input: bfloat16 [4, 32, 16, 32, 128], P('dp', 'tm', 'tile')
- weight_grad: float32 [3456, 128], P('dp')
- bias_grad: float32 [128], P('dp')
The draws below stay inside these ranges and needn't reach their ends.
All inputs are finite; a program needn't handle non-finite values.
Results may differ from the reference program's by a relative error of at most 0.0095.
Values may be sent and summed in bfloat16 or wider, within the bound.
No kernel may reach another device: no remote copies, remote signals or barrier semaphores. Data moves between devices by JAX's collectives and lax.ppermute only.
A program may use at most 64 MiB of HBM per device.

```python
import jax
import jax.numpy as jnp
from jax import lax

C = 128
COLS = 32
CLIPS = 4
FRAMES = 32
ROWS = 16
POSITIONS = 65536


def steps_of(key, extent, cuts, low, high):
    loudness = 1.0
    for dim, shards_of in cuts:
        steps = jax.random.uniform(jax.random.fold_in(jax.random.fold_in(key, 6), dim), (shards_of,), jnp.float32, low / len(cuts), high / len(cuts))
        loudness = loudness * jnp.repeat(jnp.exp(steps), extent[dim] // shards_of).reshape((-1,) + (1,) * (len(extent) - 1 - dim))
    return loudness


def gaussian(key, extent, scale, bound, cuts=(), kind=jnp.bfloat16):
    values = scale * jax.random.normal(key, extent, jnp.float32)
    if cuts:
        values = values * steps_of(key, extent, cuts, -0.22, 0.18)
    return jnp.clip(values, -bound, bound).astype(kind)


def setup_inputs(seed: int = 0) -> dict:
    seeds = jax.random.split(jax.random.key(seed), 5)
    return {
        "activations": gaussian(seeds[0], (CLIPS, FRAMES, ROWS, COLS, C), 1.0, 6.0, ((0, 4), (1, 4), (2, 2))),
        "kernel": gaussian(seeds[1], (27 * C, C), (27 * C) ** -0.5, 0.109375),
        "conv_bias": gaussian(seeds[2], (C,), 0.5, 3.0, (), jnp.float32),
        "cotangent": gaussian(seeds[3], (CLIPS, FRAMES, ROWS, COLS, C), 1.0, 6.0, ((0, 4), (1, 4), (2, 2))),
    }


def reference(activations, kernel, conv_bias, cotangent):
    channels = kernel.shape[1]
    taps = kernel.astype(jnp.float32).reshape(3, 3, 3, channels, channels)
    frames = activations.shape[1]
    height = activations.shape[2]
    breadth = activations.shape[3]
    scale = float(POSITIONS) ** -0.5

    def one_clip(carry, pair):
        weight_sum, bias_sum = carry
        video, upstream = pair
        padded = jnp.pad(video, ((2, 0), (1, 1), (1, 1), (0, 0))).astype(jnp.float32)
        running = jnp.zeros((frames, height, breadth, channels), jnp.float32) + conv_bias
        for tap_time in range(3):
            for tap_row in range(3):
                for tap_col in range(3):
                    window = padded[tap_time:tap_time + frames, tap_row:tap_row + height, tap_col:tap_col + breadth]
                    running = running + jnp.einsum("frwc,cd->frwd", window, taps[tap_time, tap_row, tap_col])
        sigma = jax.nn.sigmoid(running)
        output = (video.astype(jnp.float32) + running * sigma).astype(jnp.bfloat16)
        grad_pre = (upstream.astype(jnp.float32) * sigma * (1.0 + running * (1.0 - sigma))).astype(jnp.bfloat16)
        grad_float = grad_pre.astype(jnp.float32)
        grad_padded = jnp.pad(grad_float, ((0, 2), (1, 1), (1, 1), (0, 0)))
        back = upstream.astype(jnp.float32)
        pieces = []
        for tap_time in range(3):
            for tap_row in range(3):
                for tap_col in range(3):
                    window = grad_padded[2 - tap_time:2 - tap_time + frames, 2 - tap_row:2 - tap_row + height, 2 - tap_col:2 - tap_col + breadth]
                    back = back + jnp.einsum("frwd,cd->frwc", window, taps[tap_time, tap_row, tap_col])
                    source = padded[tap_time:tap_time + frames, tap_row:tap_row + height, tap_col:tap_col + breadth]
                    pieces.append(jnp.einsum("frwc,frwd->cd", source, grad_float))
        weight_sum = weight_sum + jnp.stack(pieces).reshape(27 * channels, channels)
        bias_sum = bias_sum + jnp.sum(grad_float, axis=(0, 1, 2))
        return (weight_sum, bias_sum), (output, back.astype(jnp.bfloat16))

    start = (jnp.zeros((27 * channels, channels), jnp.float32), jnp.zeros((channels,), jnp.float32))
    (weight_sum, bias_sum), (block_out, grad_input) = lax.scan(one_clip, start, (activations, cotangent))
    return block_out, grad_input, weight_sum * scale, bias_sum * scale
```

```python
import functools
import math

import jax
import jax.numpy as jnp
from jax import lax
from jax.experimental import pallas as pl
from jax.experimental.pallas import tpu as pltpu
from jax.sharding import PartitionSpec as P

F32 = jnp.float32
BF16 = jnp.bfloat16


def shifted_columns(cells, breadth):
    count = cells.shape[0]
    wide = cells.astype(F32)
    column = lax.broadcasted_iota(jnp.int32, cells.shape, 0) % breadth
    left = jnp.where(column == 0, 0.0, pltpu.roll(wide, 1, 0))
    right = jnp.where(column == breadth - 1, 0.0, pltpu.roll(wide, count - 1, 0))
    return left.astype(BF16), cells, right.astype(BF16)


def fill_windows(windows, frame, inner, edge, tile):
    height, breadth, channels = inner.shape
    parts = shifted_columns(inner.reshape(height * breadth, channels), breadth)
    edges = shifted_columns(edge, breadth)
    for e in range(3):
        lanes = slice(e * channels, (e + 1) * channels)
        windows[frame, 1 : height + 1, :, lanes] = parts[e].reshape(height, breadth, channels)
        rim = edges[e]
        none = jnp.zeros_like(rim)
        windows[frame, 0, :, lanes] = jnp.where(tile == 0, none, rim)
        windows[frame, height + 1, :, lanes] = jnp.where(tile == 0, rim, none)


def window_block(windows, first, height):
    blocks = []
    for f in range(4):
        for b in range(3):
            block = windows[first + f, b : b + height]
            blocks.append(block.reshape(-1, block.shape[-1]))
    return jnp.concatenate(blocks, axis=1)


def forward_kernel(
    x, edge, before, kernel, bias, cotangent, block_out, grad_pre, edge_out, *rest, arranged
):
    outs, (windows, taps, grads) = rest[:-3], rest[-3:]
    frames, height, breadth, channels = x.shape
    area = height * breadth
    tile = lax.axis_index("tile")
    rows = 9 * channels
    taps[0 : 3 * rows, 0:channels] = kernel[...]
    taps[3 * rows :, 0:channels] = jnp.zeros((rows, channels), BF16)
    taps[0:rows, channels:] = jnp.zeros((rows, channels), BF16)
    taps[rows:, channels:] = kernel[...]
    for f in range(2):
        fill_windows(windows, f, before[f * height : (f + 1) * height], before[2 * height + f], tile)
    for f in range(frames):
        fill_windows(windows, f + 2, x[f], edge[f], tile)
    both = jnp.concatenate([bias[...], bias[...]], axis=1)
    total = jnp.zeros((1, channels), F32)
    for p in range(frames // 2):
        pre = both + jnp.dot(
            window_block(windows, 2 * p, height), taps[...], preferred_element_type=F32
        )
        for s in range(2):
            t = 2 * p + s
            part = pre[:, s * channels : (s + 1) * channels]
            sigma = jax.nn.sigmoid(part)
            source = x[t].reshape(area, channels).astype(F32)
            upstream = cotangent[t].reshape(area, channels).astype(F32)
            block_out[t] = (source + part * sigma).astype(BF16).reshape(height, breadth, channels)
            grad = (upstream * sigma * (1.0 + part * (1.0 - sigma))).astype(BF16)
            grads[p * area : (p + 1) * area, s * channels : (s + 1) * channels] = grad
            total = total + jnp.sum(grad.astype(F32), axis=0, keepdims=True)
            cube = grad.reshape(height, breadth, channels)
            grad_pre[t] = cube
            edge_out[t] = jnp.where(tile == 0, cube[height - 1], cube[0])
    turned = grads[...].T
    sums = [[None] * 9 for _ in range(3)]
    for b in range(3):
        for f in range(4):
            source = jnp.concatenate(
                [
                    windows[2 * p + f, b : b + height].reshape(area, 3 * channels)
                    for p in range(frames // 2)
                ],
                axis=0,
            )
            low = 0 if f < 3 else channels
            high = 2 * channels if f > 0 else channels
            product = jnp.dot(turned[low:high], source, preferred_element_type=F32)
            for e in range(3):
                for s in range(2):
                    a = f - s
                    if 0 <= a < 3:
                        piece = product[
                            s * channels - low : (s + 1) * channels - low,
                            e * channels : (e + 1) * channels,
                        ]
                        at = b * 3 + e
                        sums[a][at] = piece if sums[a][at] is None else sums[a][at] + piece
    if not arranged:
        for a in range(3):
            for at in range(9):
                outs[0][a * 9 + at] = sums[a][at].T.astype(BF16)
        outs[1][...] = total
        return
    kept, sent = outs
    count, half = kept.shape[0], kept.shape[1]
    share = 27 * channels // count
    me = lax.axis_index("dp")
    places = [place_of(me, j, count, tile) for j in range(count)]
    theirs = [place_of(me, j, count, 1 - tile) for j in range(count)]

    def put(j, start, rows):
        done = 0
        while done < rows.shape[0]:
            h = (start + done) // half
            stop = min(rows.shape[0], (h + 1) * half - start)
            at = start + done - h * half
            piece = rows[done:stop]

            @pl.when(tile == h)
            def _():
                kept[places[j], at : at + piece.shape[0]] = piece

            @pl.when(tile != h)
            def _():
                sent[theirs[j], at : at + piece.shape[0]] = piece

            done = stop

    for k in range(27):
        block = sums[k // 9][k % 9].T.astype(BF16)
        at = k * channels
        end = at + channels
        while at < end:
            j = at // share
            stop = min(end, (j + 1) * share)
            put(j, at - j * share, block[at - k * channels : stop - k * channels])
            at = stop
    pad = 2 * half - share
    line = jnp.concatenate([total, jnp.zeros((pad - 1, channels), F32)], axis=0).astype(BF16)
    for j in range(count):
        put(j, share, line)


def input_kernel(g, edge, after, kernel, cotangent, grad_input, windows, taps):
    frames, height, breadth, channels = g.shape
    area = height * breadth
    tile = lax.axis_index("tile")
    for f in range(4):
        for s in range(2):
            a = 2 - f + s
            for b in range(3):
                for e in range(3):
                    lanes = ((f * 3 + b) * 3 + e) * channels
                    where = (slice(s * channels, (s + 1) * channels), slice(lanes, lanes + channels))
                    if 0 <= a < 3:
                        k = ((a * 3 + 2 - b) * 3 + 2 - e) * channels
                        taps[where] = kernel[k : k + channels]
                    else:
                        taps[where] = jnp.zeros((channels, channels), BF16)
    for f in range(frames):
        fill_windows(windows, f, g[f], edge[f], tile)
    for f in range(2):
        fill_windows(
            windows, frames + f, after[f * height : (f + 1) * height], after[2 * height + f], tile
        )
    for p in range(frames // 2):
        back = lax.dot_general(
            window_block(windows, 2 * p, height),
            taps[...],
            (((1,), (1,)), ((), ())),
            preferred_element_type=F32,
        )
        for s in range(2):
            t = 2 * p + s
            part = back[:, s * channels : (s + 1) * channels].reshape(height, breadth, channels)
            grad_input[t] = (cotangent[t].astype(F32) + part).astype(BF16)


def bits_of(count):
    return count.bit_length() - 1


def place_of(me, shard, count, tile):
    apart = me ^ shard
    n = bits_of(count)
    plain = apart * 0
    turned = apart * 0
    for k in range(n):
        bit = (apart >> k) & 1
        plain = plain | (bit << (n - 1 - k))
        turned = turned | (bit << k)
    return jnp.where(tile == 0, plain, turned)


def exchange(block, axis, count, bits):
    route = []
    for i in range(count):
        for c in range(2):
            route.append((i * 2 + c, (i ^ bits[c]) * 2 + c))
    return lax.ppermute(block, (axis, "tile"), route)


def added(a, b):
    return (a.astype(F32) + b.astype(F32)).astype(BF16)


def passed_along(block, axis, distance):
    count = lax.axis_size(axis)
    route = [(i - distance, i) for i in range(count) if 0 <= i - distance < count]
    return lax.ppermute(block, axis, route)


def swapped(block):
    return lax.ppermute(block, "tile", [(0, 1), (1, 0)])


def body(activations, kernel, conv_bias, cotangent):
    clip_count, frames, height, breadth, channels = activations.shape
    x, upstream = activations[0], cotangent[0]
    tile = lax.axis_index("tile")
    shards = lax.axis_size("dp")
    steps = lax.axis_size("tm")
    share = 27 * channels // shards
    half = -(-(share + 1) // 32) * 16
    arranged = share % 32 == 0

    edge = swapped(jnp.where(tile == 0, x[:, height - 1], x[:, 0]))
    before = passed_along(
        jnp.concatenate(
            [x[frames - 2 :].reshape(2 * height, breadth, channels), edge[frames - 2 :]], axis=0
        ),
        "tm",
        1,
    )
    cells = jax.ShapeDtypeStruct(x.shape, BF16)
    lines = jax.ShapeDtypeStruct((frames, breadth, channels), BF16)
    if arranged:
        partial = [jax.ShapeDtypeStruct((shards, half, channels), BF16)] * 2
    else:
        partial = [
            jax.ShapeDtypeStruct((27, channels, channels), BF16),
            jax.ShapeDtypeStruct((1, channels), F32),
        ]
    scratch = [pltpu.VMEM((frames + 2, height + 2, breadth, 3 * channels), BF16)]
    block_out, grad_pre, grad_edge, *parts = pl.pallas_call(
        functools.partial(forward_kernel, arranged=arranged),
        out_shape=[cells, cells, lines] + partial,
        scratch_shapes=scratch
        + [
            pltpu.VMEM((36 * channels, 2 * channels), BF16),
            pltpu.VMEM((frames // 2 * height * breadth, 2 * channels), BF16),
        ],
        compiler_params=pltpu.CompilerParams(vmem_limit_bytes=40 * 2**20),
        name="forward_and_weights",
    )(x, edge, before, kernel, conv_bias.reshape(1, channels), upstream)
    if arranged:
        kept, sent = parts
    else:
        weight = parts[0].reshape(shards, share, channels)
        line = jnp.broadcast_to(parts[1].astype(BF16)[None], (shards, 1, channels))
        pad = jnp.zeros((shards, 2 * half - share - 1, channels), BF16)
        whole = jnp.concatenate([weight, line, pad], axis=1)
        me = lax.axis_index("dp")
        whole = whole.reshape(shards, 2, half, channels)
        kept, sent = (
            jnp.zeros((shards, half, channels), BF16)
            .at[place_of(me, jnp.arange(shards), shards, side)]
            .set(lax.dynamic_index_in_dim(whole, side, 1, False))
            for side in (tile, 1 - tile)
        )

    total = added(kept, swapped(sent))
    n = bits_of(shards)
    for k in range(n):
        middle = total.shape[0] // 2
        total = added(
            total[:middle], exchange(total[middle:], "dp", shards, (1 << k, 1 << (n - 1 - k)))
        )
    total = total[0]
    n = bits_of(steps)
    for k in range(n):
        total = added(total, exchange(total, "tm", steps, (1 << k, 1 << (n - 1 - k))))
    other = swapped(total)
    whole = jnp.where(
        tile == 0,
        jnp.concatenate([total, other], axis=0),
        jnp.concatenate([other, total], axis=0),
    ).astype(F32)

    edge = swapped(grad_edge)
    after = passed_along(
        jnp.concatenate(
            [grad_pre[:2].reshape(2 * height, breadth, channels), edge[:2]], axis=0
        ),
        "tm",
        -1,
    )
    grad_input = pl.pallas_call(
        input_kernel,
        out_shape=cells,
        scratch_shapes=scratch + [pltpu.VMEM((2 * channels, 36 * channels), BF16)],
        compiler_params=pltpu.CompilerParams(vmem_limit_bytes=32 * 2**20),
        cost_estimate=pl.CostEstimate(
            flops=2 * 27 * channels * channels * frames * height * breadth,
            bytes_accessed=8 * 2**20,
            transcendentals=0,
        ),
        name="input_gradient",
    )(grad_pre, edge, after, kernel, upstream)

    positions = (
        clip_count * frames * height * breadth * shards * steps * lax.axis_size("tile")
    )
    scale = 1.0 / math.sqrt(positions)
    bias_share = channels // shards
    bias_row = lax.dynamic_slice_in_dim(
        whole[share], lax.axis_index("dp") * bias_share, bias_share, 0
    )
    return block_out[None], grad_input[None], whole[:share] * scale, bias_row * scale


def solution(mesh):
    return jax.shard_map(
        body,
        mesh=mesh,
        in_specs=(P("dp", "tm", "tile", None, None), P(), P(), P("dp", "tm", "tile", None, None)),
        out_specs=(
            P("dp", "tm", "tile", None, None),
            P("dp", "tm", "tile", None, None),
            P("dp", None),
            P("dp"),
        ),
        check_vma=False,
    )
```

```python
import functools
import math

import jax
import jax.numpy as jnp
from jax import lax
from jax.experimental import pallas as pl
from jax.experimental.pallas import tpu as pltpu
from jax.sharding import PartitionSpec as P

F32 = jnp.float32
BF16 = jnp.bfloat16


def shifted_columns(cells, breadth):
    count = cells.shape[0]
    wide = cells.astype(F32)
    column = lax.broadcasted_iota(jnp.int32, cells.shape, 0) % breadth
    left = jnp.where(column == 0, 0.0, pltpu.roll(wide, 1, 0))
    right = jnp.where(column == breadth - 1, 0.0, pltpu.roll(wide, count - 1, 0))
    return left.astype(BF16), cells, right.astype(BF16)


def fill_windows(windows, frame, inner, edge, tile):
    height, breadth, channels = inner.shape
    parts = shifted_columns(inner.reshape(height * breadth, channels), breadth)
    edges = shifted_columns(edge, breadth)
    for e in range(3):
        lanes = slice(e * channels, (e + 1) * channels)
        windows[frame, 1 : height + 1, :, lanes] = parts[e].reshape(height, breadth, channels)
        rim = edges[e]
        none = jnp.zeros_like(rim)
        windows[frame, 0, :, lanes] = jnp.where(tile == 0, none, rim)
        windows[frame, height + 1, :, lanes] = jnp.where(tile == 0, rim, none)


def window_rows(pieces, frame, b, height):
    for first, ref in pieces:
        if first <= frame < first + ref.shape[0]:
            block = ref[frame - first, b : b + height]
            return block.reshape(-1, block.shape[-1])


def window_block(pieces, first, height):
    return jnp.concatenate(
        [window_rows(pieces, first + f, b, height) for f in range(4) for b in range(3)], axis=1
    )


def activate(pre, source, upstream):
    sigma = jax.nn.sigmoid(pre)
    result = (source.astype(F32) + pre * sigma).astype(BF16)
    grad = (upstream.astype(F32) * sigma * (1.0 + pre * (1.0 - sigma))).astype(BF16)
    return result, grad


def forward_pair(pieces, p, taps, bias, x_pair, upstream, height):
    channels = bias.shape[1]
    both = jnp.concatenate([bias[...], bias[...]], axis=1)
    pre = both + jnp.dot(
        window_block(pieces, 2 * p, height), taps[...], preferred_element_type=F32
    )
    return [
        activate(
            pre[:, s * channels : (s + 1) * channels],
            x_pair[s].reshape(-1, channels),
            upstream[s].reshape(-1, channels),
        )
        for s in range(2)
    ]


def interior_kernel(
    x,
    edge,
    kernel,
    bias,
    cotangent,
    block_out,
    windows,
    taps,
    turned,
    grad_pre,
    edge_out,
    total,
    bias_here,
    upstream,
    result,
    arriving,
    leaving,
):
    frames, height, breadth, channels = x.shape
    area = height * breadth
    tile = lax.axis_index("tile")
    bias_copy = pltpu.make_async_copy(bias, bias_here, arriving.at[0])
    up_copy = pltpu.make_async_copy(cotangent.at[2:frames], upstream, arriving.at[1])
    bias_copy.start()
    up_copy.start()
    rows = 9 * channels
    taps[0 : 3 * rows, 0:channels] = kernel[...]
    taps[3 * rows :, 0:channels] = jnp.zeros((rows, channels), BF16)
    taps[0:rows, channels:] = jnp.zeros((rows, channels), BF16)
    taps[rows:, channels:] = kernel[...]
    for f in range(frames):
        fill_windows(windows, f, x[f], edge[f], tile)
    bias_copy.wait()
    up_copy.wait()
    summed = jnp.zeros((1, channels), F32)
    copies = []
    for p in range(1, frames // 2):
        grads = []
        outs = forward_pair(
            [(2, windows)],
            p,
            taps,
            bias_here,
            [x[2 * p], x[2 * p + 1]],
            [upstream[2 * p - 2], upstream[2 * p - 1]],
            height,
        )
        for s in range(2):
            t = 2 * p + s - 2
            result[t] = outs[s][0].reshape(height, breadth, channels)
            grad = outs[s][1]
            grads.append(grad)
            summed = summed + jnp.sum(grad.astype(F32), axis=0, keepdims=True)
            cube = grad.reshape(height, breadth, channels)
            grad_pre[t] = cube
            edge_out[t] = jnp.where(tile == 0, cube[height - 1], cube[0])
        turned[:, (p - 1) * area : p * area] = jnp.concatenate(grads, axis=1).T
        copy = pltpu.make_async_copy(
            result.at[2 * p - 2 : 2 * p], block_out.at[2 * p : 2 * p + 2], leaving.at[p - 1]
        )
        copy.start()
        copies.append(copy)
    total[...] = summed
    for copy in copies:
        copy.wait()


def first_frames_kernel(
    block_in,
    x,
    edge,
    before,
    bias,
    cotangent,
    windows,
    taps,
    turned,
    edge_in,
    total,
    block_out,
    grad_pre,
    edge_out,
    *rest,
    arranged,
):
    outs, (early, bias_here, upstream, result, arriving, leaving) = rest[:-6], rest[-6:]
    frames, height, breadth, channels = x.shape
    area = height * breadth
    tile = lax.axis_index("tile")
    bias_copy = pltpu.make_async_copy(bias, bias_here, arriving.at[0])
    up_copy = pltpu.make_async_copy(cotangent.at[0:2], upstream, arriving.at[1])
    bias_copy.start()
    up_copy.start()
    for f in range(2):
        fill_windows(early, f, before[f * height : (f + 1) * height], before[2 * height + f], tile)
    bias_copy.wait()
    up_copy.wait()
    pieces = [(0, early), (2, windows)]
    summed = total[...]
    firsts = forward_pair(
        pieces, 0, taps, bias_here, [x[0], x[1]], [upstream[0], upstream[1]], height
    )
    for s in range(2):
        result[s] = firsts[s][0].reshape(height, breadth, channels)
        cube = firsts[s][1].reshape(height, breadth, channels)
        summed = summed + jnp.sum(firsts[s][1].astype(F32), axis=0, keepdims=True)
        grad_pre[s] = cube
        edge_out[s] = jnp.where(tile == 0, cube[height - 1], cube[0])
    edge_out[2:frames] = edge_in[...]
    copy = pltpu.make_async_copy(result, block_out.at[0:2], leaving)
    copy.start()
    grads = jnp.concatenate(
        [jnp.concatenate([firsts[0][1], firsts[1][1]], axis=1).T, turned[...]], axis=1
    )
    sums = [[None] * 9 for _ in range(3)]
    for b in range(3):
        for f in range(4):
            source = jnp.concatenate(
                [window_rows(pieces, 2 * p + f, b, height) for p in range(frames // 2)], axis=0
            )
            low = 0 if f < 3 else channels
            high = 2 * channels if f > 0 else channels
            product = jnp.dot(grads[low:high], source, preferred_element_type=F32)
            for e in range(3):
                for s in range(2):
                    a = f - s
                    if 0 <= a < 3:
                        piece = product[
                            s * channels - low : (s + 1) * channels - low,
                            e * channels : (e + 1) * channels,
                        ]
                        at = b * 3 + e
                        sums[a][at] = piece if sums[a][at] is None else sums[a][at] + piece
    if not arranged:
        for k in range(27):
            outs[0][k] = sums[k // 9][k % 9].T.astype(BF16)
        outs[1][...] = summed
        copy.wait()
        return
    (parts,) = outs
    count, half = parts.shape[1], parts.shape[2]
    share = 27 * channels // count
    me = lax.axis_index("dp")

    def put(j, start, rows):
        done = 0
        while done < rows.shape[0]:
            h = (start + done) // half
            stop = min(rows.shape[0], (h + 1) * half - start)
            at = start + done - h * half
            place = place_of(me, j, count, h)
            parts[tile ^ h, place, at : at + stop - done] = rows[done:stop]
            done = stop

    for k in range(27):
        block = sums[k // 9][k % 9].astype(BF16).T
        at = k * channels
        end = at + channels
        while at < end:
            j = at // share
            stop = min(end, (j + 1) * share)
            put(j, at - j * share, block[at - k * channels : stop - k * channels])
            at = stop
    pad = 2 * half - share
    line = jnp.concatenate([summed, jnp.zeros((pad - 1, channels), F32)], axis=0).astype(BF16)
    for j in range(count):
        put(j, share, line)
    copy.wait()


def back_pair(pieces, p, taps, upstream, height):
    back = lax.dot_general(
        window_block(pieces, 2 * p, height),
        taps[...],
        (((1,), (1,)), ((), ())),
        preferred_element_type=F32,
    )
    channels = back.shape[1] // 2
    return [
        (
            upstream[s].astype(F32)
            + back[:, s * channels : (s + 1) * channels].reshape(upstream[s].shape)
        ).astype(BF16)
        for s in range(2)
    ]


def back_interior_kernel(
    early, g, edge, kernel, cotangent, grad_input, last, taps, windows, upstream, result, arriving, leaving
):
    frames, height, breadth, channels = cotangent.shape
    tile = lax.axis_index("tile")
    up_copy = pltpu.make_async_copy(cotangent.at[0 : frames - 2], upstream, arriving)
    up_copy.start()
    for f in range(4):
        for s in range(2):
            a = 2 - f + s
            for b in range(3):
                for e in range(3):
                    lanes = ((f * 3 + b) * 3 + e) * channels
                    where = (slice(s * channels, (s + 1) * channels), slice(lanes, lanes + channels))
                    if 0 <= a < 3:
                        k = ((a * 3 + 2 - b) * 3 + 2 - e) * channels
                        taps[where] = kernel[k : k + channels]
                    else:
                        taps[where] = jnp.zeros((channels, channels), BF16)
    for f in range(frames):
        cells = early[f] if f < 2 else g[f - 2]
        if f < frames - 2:
            fill_windows(windows, f, cells, edge[f], tile)
        else:
            fill_windows(last, f - (frames - 2), cells, edge[f], tile)
    up_copy.wait()
    copies = []
    for p in range(frames // 2 - 1):
        pair = back_pair(
            [(0, windows), (frames - 2, last)],
            p,
            taps,
            [upstream[2 * p], upstream[2 * p + 1]],
            height,
        )
        for s in range(2):
            result[2 * p + s] = pair[s]
        copy = pltpu.make_async_copy(
            result.at[2 * p : 2 * p + 2], grad_input.at[2 * p : 2 * p + 2], leaving.at[p]
        )
        copy.start()
        copies.append(copy)
    for copy in copies:
        copy.wait()


def back_last_kernel(
    grad_in, last, after, taps, cotangent, grad_input, windows, upstream, result, arriving, leaving
):
    frames, height, breadth, channels = cotangent.shape
    tile = lax.axis_index("tile")
    up_copy = pltpu.make_async_copy(cotangent.at[frames - 2 : frames], upstream, arriving)
    up_copy.start()
    for f in range(2):
        fill_windows(windows, f, after[f * height : (f + 1) * height], after[2 * height + f], tile)
    up_copy.wait()
    pair = back_pair(
        [(frames - 2, last), (frames, windows)],
        frames // 2 - 1,
        taps,
        [upstream[0], upstream[1]],
        height,
    )
    for s in range(2):
        result[s] = pair[s]
    copy = pltpu.make_async_copy(result, grad_input.at[frames - 2 : frames], leaving)
    copy.start()
    copy.wait()


def bits_of(count):
    return count.bit_length() - 1


def place_of(me, shard, count, tile):
    apart = me ^ shard
    n = bits_of(count)
    plain = apart * 0
    turned = apart * 0
    for k in range(n):
        bit = (apart >> k) & 1
        plain = plain | (bit << (n - 1 - k))
        turned = turned | (bit << k)
    return jnp.where(tile == 0, plain, turned)


def exchange(block, axis, count, bits):
    route = []
    for i in range(count):
        for c in range(2):
            route.append((i * 2 + c, (i ^ bits[c]) * 2 + c))
    return lax.ppermute(block, (axis, "tile"), route)


def added(a, b):
    return (a.astype(F32) + b.astype(F32)).astype(BF16)


def passed_along(block, axis, distance):
    count = lax.axis_size(axis)
    route = [(i - distance, i) for i in range(count) if 0 <= i - distance < count]
    return lax.ppermute(block, axis, route)


def swapped(block):
    return lax.ppermute(block, "tile", [(0, 1), (1, 0)])


def body(activations, kernel, conv_bias, cotangent):
    clip_count, frames, height, breadth, channels = activations.shape
    x, upstream = activations[0], cotangent[0]
    tile = lax.axis_index("tile")
    shards = lax.axis_size("dp")
    steps = lax.axis_size("tm")
    share = 27 * channels // shards
    half = -(-(share + 1) // 32) * 16
    arranged = share % 32 == 0

    row = jnp.where(tile == 0, height - 1, 0)
    edge = swapped(lax.dynamic_index_in_dim(x, row, 1, False))
    before = passed_along(
        jnp.concatenate(
            [x[frames - 2 :].reshape(2 * height, breadth, channels), edge[frames - 2 :]], axis=0
        ),
        "tm",
        1,
    )
    area = height * breadth
    bias = conv_bias.reshape(1, channels)
    cells = jax.ShapeDtypeStruct(x.shape, BF16)

    def arrays(*shapes, kind=BF16):
        return [jax.ShapeDtypeStruct(shape, kind) for shape in shapes]

    def windows_shape(count):
        return (count, height + 2, breadth, 3 * channels)

    def frames_shape(count):
        return (count, height, breadth, channels)

    def call(kernel_body, name, share, shapes, scratch, far_in, far_out, args, aliases=None):
        here, there = pl.BlockSpec(memory_space=pltpu.VMEM), pl.BlockSpec(memory_space=pltpu.HBM)
        return pl.pallas_call(
            kernel_body,
            out_shape=shapes,
            in_specs=[there if i in far_in else here for i in range(len(args))],
            out_specs=[there if i in far_out else here for i in range(len(shapes))],
            scratch_shapes=scratch,
            input_output_aliases=aliases or {},
            compiler_params=pltpu.CompilerParams(vmem_limit_bytes=32 * 2**20),
            cost_estimate=pl.CostEstimate(
                flops=int(share * 4 * 27 * channels * channels * frames * area),
                bytes_accessed=4 * 2**20,
                transcendentals=0,
            ),
            name=name,
        )(*args)

    dma, vmem = pltpu.SemaphoreType.DMA, pltpu.VMEM
    block_out, windows, taps, turned, later_grads, later_edge, total = call(
        interior_kernel,
        "forward_interior",
        0.75,
        [cells]
        + arrays(
            windows_shape(frames),
            (36 * channels, 2 * channels),
            (2 * channels, (frames // 2 - 1) * area),
            frames_shape(frames - 2),
            (frames - 2, breadth, channels),
        )
        + arrays((1, channels), kind=F32),
        [
            vmem((1, channels), F32),
            vmem(frames_shape(frames - 2), BF16),
            vmem(frames_shape(frames - 2), BF16),
            dma((2,)),
            dma((frames // 2 - 1,)),
        ],
        (3, 4),
        (0,),
        (x, edge, kernel, bias, upstream),
    )
    if arranged:
        partial = arrays((2, shards, half, channels))
    else:
        partial = arrays((27, channels, channels)) + arrays((1, channels), kind=F32)
    block_out, early_grads, grad_edge, *parts = call(
        functools.partial(first_frames_kernel, arranged=arranged),
        "first_frames_and_weights",
        1.25,
        [cells] + arrays(frames_shape(2), (frames, breadth, channels)) + partial,
        [
            vmem(windows_shape(2), BF16),
            vmem((1, channels), F32),
            vmem(frames_shape(2), BF16),
            vmem(frames_shape(2), BF16),
            dma((2,)),
            dma,
        ],
        (0, 4, 5),
        (0,),
        (
            block_out,
            x,
            edge,
            before,
            bias,
            upstream,
            windows,
            taps,
            turned,
            later_edge,
            total,
        ),
        {0: 0},
    )
    if arranged:
        kept, sent = parts[0][0], parts[0][1]
    else:
        weight = parts[0].reshape(shards, share, channels)
        line = jnp.broadcast_to(parts[1].astype(BF16)[None], (shards, 1, channels))
        pad = jnp.zeros((shards, 2 * half - share - 1, channels), BF16)
        whole = jnp.concatenate([weight, line, pad], axis=1)
        me = lax.axis_index("dp")
        whole = whole.reshape(shards, 2, half, channels)
        kept, sent = (
            jnp.zeros((shards, half, channels), BF16)
            .at[place_of(me, jnp.arange(shards), shards, side)]
            .set(lax.dynamic_index_in_dim(whole, side, 1, False))
            for side in (tile, 1 - tile)
        )

    total = added(kept, swapped(sent))
    edge = swapped(grad_edge)
    after = passed_along(
        jnp.concatenate(
            [early_grads.reshape(2 * height, breadth, channels), edge[:2]], axis=0
        ),
        "tm",
        -1,
    )
    grad_input, last, taps = call(
        back_interior_kernel,
        "input_gradient_interior",
        0.75,
        [cells] + arrays(windows_shape(2), (2 * channels, 36 * channels)),
        [
            vmem(windows_shape(frames - 2), BF16),
            vmem(frames_shape(frames - 2), BF16),
            vmem(frames_shape(frames - 2), BF16),
            dma,
            dma((frames // 2 - 1,)),
        ],
        (4,),
        (0,),
        (early_grads, later_grads, edge, kernel, upstream),
    )
    n = bits_of(shards)
    for k in range(n):
        if k == n - 1:
            total, grad_input = lax.optimization_barrier((total, grad_input))
        middle = total.shape[0] // 2
        total = added(
            total[:middle], exchange(total[middle:], "dp", shards, (1 << k, 1 << (n - 1 - k)))
        )
    (grad_input,) = call(
        back_last_kernel,
        "input_gradient_last",
        0.25,
        [cells],
        [
            vmem(windows_shape(2), BF16),
            vmem(frames_shape(2), BF16),
            vmem(frames_shape(2), BF16),
            dma,
            dma,
        ],
        (0, 4),
        (0,),
        (grad_input, last, after, taps, upstream),
        {0: 0},
    )
    total = total[0]
    n = bits_of(steps)
    for k in range(n):
        if k == n - 1:
            total, grad_input = lax.optimization_barrier((total, grad_input))
        total = added(total, exchange(total, "tm", steps, (1 << k, 1 << (n - 1 - k))))
    other = swapped(total)
    whole = jnp.where(
        tile == 0,
        jnp.concatenate([total, other], axis=0),
        jnp.concatenate([other, total], axis=0),
    ).astype(F32)

    positions = (
        clip_count * frames * height * breadth * shards * steps * lax.axis_size("tile")
    )
    scale = 1.0 / math.sqrt(positions)
    bias_share = channels // shards
    bias_row = lax.dynamic_slice_in_dim(
        whole[share], lax.axis_index("dp") * bias_share, bias_share, 0
    )
    return block_out[None], grad_input[None], whole[:share] * scale, bias_row * scale


def solution(mesh):
    return jax.shard_map(
        body,
        mesh=mesh,
        in_specs=(P("dp", "tm", "tile", None, None), P(), P(), P("dp", "tm", "tile", None, None)),
        out_specs=(
            P("dp", "tm", "tile", None, None),
            P("dp", "tm", "tile", None, None),
            P("dp", None),
            P("dp"),
        ),
        check_vma=False,
    )
```

```python
import functools
import math

import jax
import jax.numpy as jnp
from jax import lax
from jax.experimental import pallas as pl
from jax.experimental.pallas import tpu as pltpu
from jax.sharding import PartitionSpec as P

F32 = jnp.float32
BF16 = jnp.bfloat16


def shifted_columns(cells, breadth):
    count = cells.shape[0]
    wide = cells.astype(F32)
    column = lax.broadcasted_iota(jnp.int32, cells.shape, 0) % breadth
    left = jnp.where(column == 0, 0.0, pltpu.roll(wide, 1, 0))
    right = jnp.where(column == breadth - 1, 0.0, pltpu.roll(wide, count - 1, 0))
    return left.astype(BF16), cells, right.astype(BF16)


def fill_windows(windows, frame, inner, edge, tile):
    height, breadth, channels = inner.shape
    parts = shifted_columns(inner.reshape(height * breadth, channels), breadth)
    edges = shifted_columns(edge, breadth)
    for e in range(3):
        lanes = slice(e * channels, (e + 1) * channels)
        windows[frame, 1 : height + 1, :, lanes] = parts[e].reshape(height, breadth, channels)
        rim = edges[e]
        none = jnp.zeros_like(rim)
        windows[frame, 0, :, lanes] = jnp.where(tile == 0, none, rim)
        windows[frame, height + 1, :, lanes] = jnp.where(tile == 0, rim, none)


def window_rows(pieces, frame, b, height):
    for first, ref in pieces:
        if first <= frame < first + ref.shape[0]:
            block = ref[frame - first, b : b + height]
            return block.reshape(-1, block.shape[-1])


def window_block(pieces, first, height):
    return jnp.concatenate(
        [window_rows(pieces, first + f, b, height) for f in range(4) for b in range(3)], axis=1
    )


def activate(pre, source, upstream):
    sigma = jax.nn.sigmoid(pre)
    result = (source.astype(F32) + pre * sigma).astype(BF16)
    grad = (upstream.astype(F32) * sigma * (1.0 + pre * (1.0 - sigma))).astype(BF16)
    return result, grad


def forward_pair(pieces, p, taps, bias, x_pair, upstream, height):
    channels = bias.shape[1]
    both = jnp.concatenate([bias[...], bias[...]], axis=1)
    pre = both + jnp.dot(
        window_block(pieces, 2 * p, height), taps[...], preferred_element_type=F32
    )
    return [
        activate(
            pre[:, s * channels : (s + 1) * channels],
            x_pair[s].reshape(-1, channels),
            upstream[s].reshape(-1, channels),
        )
        for s in range(2)
    ]


def interior_kernel(
    x,
    edge,
    kernel,
    bias,
    cotangent,
    block_out,
    windows,
    taps,
    turned,
    grad_pre,
    edge_out,
    total,
    bias_here,
    upstream,
    result,
    arriving,
    leaving,
):
    frames, height, breadth, channels = x.shape
    area = height * breadth
    tile = lax.axis_index("tile")
    bias_copy = pltpu.make_async_copy(bias, bias_here, arriving.at[0])
    up_copy = pltpu.make_async_copy(cotangent.at[2:frames], upstream, arriving.at[1])
    bias_copy.start()
    up_copy.start()
    rows = 9 * channels
    taps[0 : 3 * rows, 0:channels] = kernel[...]
    taps[3 * rows :, 0:channels] = jnp.zeros((rows, channels), BF16)
    taps[0:rows, channels:] = jnp.zeros((rows, channels), BF16)
    taps[rows:, channels:] = kernel[...]
    for f in range(frames):
        fill_windows(windows, f, x[f], edge[f], tile)
    bias_copy.wait()
    up_copy.wait()
    summed = jnp.zeros((1, channels), F32)
    copies = []
    for p in range(1, frames // 2):
        grads = []
        outs = forward_pair(
            [(2, windows)],
            p,
            taps,
            bias_here,
            [x[2 * p], x[2 * p + 1]],
            [upstream[2 * p - 2], upstream[2 * p - 1]],
            height,
        )
        for s in range(2):
            t = 2 * p + s - 2
            result[t] = outs[s][0].reshape(height, breadth, channels)
            grad = outs[s][1]
            grads.append(grad)
            summed = summed + jnp.sum(grad.astype(F32), axis=0, keepdims=True)
            cube = grad.reshape(height, breadth, channels)
            grad_pre[t] = cube
            edge_out[t] = jnp.where(tile == 0, cube[height - 1], cube[0])
        turned[:, (p - 1) * area : p * area] = jnp.concatenate(grads, axis=1).T
        copy = pltpu.make_async_copy(
            result.at[2 * p - 2 : 2 * p], block_out.at[2 * p : 2 * p + 2], leaving.at[p - 1]
        )
        copy.start()
        copies.append(copy)
    total[...] = summed
    for copy in copies:
        copy.wait()


def first_frames_kernel(
    block_in,
    x,
    edge,
    before,
    bias,
    cotangent,
    windows,
    taps,
    turned,
    edge_in,
    total,
    block_out,
    grad_pre,
    edge_out,
    *rest,
    arranged,
):
    outs, (early, bias_here, upstream, result, arriving, leaving) = rest[:-6], rest[-6:]
    frames, height, breadth, channels = x.shape
    area = height * breadth
    tile = lax.axis_index("tile")
    bias_copy = pltpu.make_async_copy(bias, bias_here, arriving.at[0])
    up_copy = pltpu.make_async_copy(cotangent.at[0:2], upstream, arriving.at[1])
    bias_copy.start()
    up_copy.start()
    for f in range(2):
        fill_windows(early, f, before[f * height : (f + 1) * height], before[2 * height + f], tile)
    bias_copy.wait()
    up_copy.wait()
    pieces = [(0, early), (2, windows)]
    summed = total[...]
    firsts = forward_pair(
        pieces, 0, taps, bias_here, [x[0], x[1]], [upstream[0], upstream[1]], height
    )
    for s in range(2):
        result[s] = firsts[s][0].reshape(height, breadth, channels)
        cube = firsts[s][1].reshape(height, breadth, channels)
        summed = summed + jnp.sum(firsts[s][1].astype(F32), axis=0, keepdims=True)
        grad_pre[s] = cube
        edge_out[s] = jnp.where(tile == 0, cube[height - 1], cube[0])
    edge_out[2:frames] = edge_in[...]
    copy = pltpu.make_async_copy(result, block_out.at[0:2], leaving)
    copy.start()
    grads = jnp.concatenate(
        [jnp.concatenate([firsts[0][1], firsts[1][1]], axis=1).T, turned[...]], axis=1
    )
    sums = [[None] * 9 for _ in range(3)]
    for b in range(3):
        for f in range(4):
            source = jnp.concatenate(
                [window_rows(pieces, 2 * p + f, b, height) for p in range(frames // 2)], axis=0
            )
            low = 0 if f < 3 else channels
            high = 2 * channels if f > 0 else channels
            product = jnp.dot(grads[low:high], source, preferred_element_type=F32)
            for e in range(3):
                for s in range(2):
                    a = f - s
                    if 0 <= a < 3:
                        piece = product[
                            s * channels - low : (s + 1) * channels - low,
                            e * channels : (e + 1) * channels,
                        ]
                        at = b * 3 + e
                        sums[a][at] = piece if sums[a][at] is None else sums[a][at] + piece
    if not arranged:
        for k in range(27):
            outs[0][k] = sums[k // 9][k % 9].T.astype(BF16)
        outs[1][...] = summed
        copy.wait()
        return
    (parts,) = outs
    count, half = parts.shape[1], parts.shape[2]
    share = 27 * channels // count
    me = lax.axis_index("dp")

    def put(j, start, rows):
        done = 0
        while done < rows.shape[0]:
            h = (start + done) // half
            stop = min(rows.shape[0], (h + 1) * half - start)
            at = start + done - h * half
            place = place_of(me, j, count, h)
            parts[tile ^ h, place, at : at + stop - done] = rows[done:stop]
            done = stop

    for k in range(27):
        block = sums[k // 9][k % 9].astype(BF16).T
        at = k * channels
        end = at + channels
        while at < end:
            j = at // share
            stop = min(end, (j + 1) * share)
            put(j, at - j * share, block[at - k * channels : stop - k * channels])
            at = stop
    pad = 2 * half - share
    line = jnp.concatenate([summed, jnp.zeros((pad - 1, channels), F32)], axis=0).astype(BF16)
    for j in range(count):
        put(j, share, line)
    copy.wait()


def back_pair(pieces, p, taps, upstream, height):
    back = lax.dot_general(
        window_block(pieces, 2 * p, height),
        taps[...],
        (((1,), (1,)), ((), ())),
        preferred_element_type=F32,
    )
    channels = back.shape[1] // 2
    return [
        (
            upstream[s].astype(F32)
            + back[:, s * channels : (s + 1) * channels].reshape(upstream[s].shape)
        ).astype(BF16)
        for s in range(2)
    ]


def back_interior_kernel(
    early, g, edge, kernel, cotangent, grad_input, last, taps, windows, upstream, result, arriving, leaving
):
    frames, height, breadth, channels = cotangent.shape
    tile = lax.axis_index("tile")
    up_copy = pltpu.make_async_copy(cotangent.at[0 : frames - 2], upstream, arriving)
    up_copy.start()
    for f in range(4):
        for s in range(2):
            a = 2 - f + s
            for b in range(3):
                for e in range(3):
                    lanes = ((f * 3 + b) * 3 + e) * channels
                    where = (slice(s * channels, (s + 1) * channels), slice(lanes, lanes + channels))
                    if 0 <= a < 3:
                        k = ((a * 3 + 2 - b) * 3 + 2 - e) * channels
                        taps[where] = kernel[k : k + channels]
                    else:
                        taps[where] = jnp.zeros((channels, channels), BF16)
    for f in range(frames):
        cells = early[f] if f < 2 else g[f - 2]
        if f < frames - 2:
            fill_windows(windows, f, cells, edge[f], tile)
        else:
            fill_windows(last, f - (frames - 2), cells, edge[f], tile)
    up_copy.wait()
    copies = []
    for p in range(frames // 2 - 1):
        pair = back_pair(
            [(0, windows), (frames - 2, last)],
            p,
            taps,
            [upstream[2 * p], upstream[2 * p + 1]],
            height,
        )
        for s in range(2):
            result[2 * p + s] = pair[s]
        copy = pltpu.make_async_copy(
            result.at[2 * p : 2 * p + 2], grad_input.at[2 * p : 2 * p + 2], leaving.at[p]
        )
        copy.start()
        copies.append(copy)
    for copy in copies:
        copy.wait()


def back_last_kernel(
    grad_in, last, after, taps, cotangent, grad_input, windows, upstream, result, arriving, leaving
):
    frames, height, breadth, channels = cotangent.shape
    tile = lax.axis_index("tile")
    up_copy = pltpu.make_async_copy(cotangent.at[frames - 2 : frames], upstream, arriving)
    up_copy.start()
    for f in range(2):
        fill_windows(windows, f, after[f * height : (f + 1) * height], after[2 * height + f], tile)
    up_copy.wait()
    pair = back_pair(
        [(frames - 2, last), (frames, windows)],
        frames // 2 - 1,
        taps,
        [upstream[0], upstream[1]],
        height,
    )
    for s in range(2):
        result[s] = pair[s]
    copy = pltpu.make_async_copy(result, grad_input.at[frames - 2 : frames], leaving)
    copy.start()
    copy.wait()


def border_kernel(x, edge, tail, copied):
    frames, height = x.shape[:2]
    row = jnp.where(lax.axis_index("tile") == 0, height - 1, 0)
    copies = [
        pltpu.make_async_copy(x.at[:, row], edge, copied.at[0]),
        pltpu.make_async_copy(x.at[frames - 2 : frames], tail, copied.at[1]),
    ]
    for copy in copies:
        copy.start()
    for copy in copies:
        copy.wait()


def closing_kernel(own, other, weight, bias, *, scale):
    tile = lax.axis_index("tile")
    half, channels = own.shape
    rest = weight.shape[0] - half
    mine, theirs = own[...].astype(F32) * scale, other[...].astype(F32) * scale
    first = jnp.where(tile == 0, mine, theirs)
    second = jnp.where(tile == 0, theirs, mine)
    weight[0:half] = first
    weight[half:] = second[0:rest]
    line = second[rest : rest + 1]
    share = bias.shape[1]
    spot = lax.axis_index("dp") * share
    picked = jnp.zeros((1, share), F32)
    for j in range(channels // share):
        picked = jnp.where(spot == j * share, line[:, j * share : (j + 1) * share], picked)
    bias[...] = picked


def bits_of(count):
    return count.bit_length() - 1


def place_of(me, shard, count, tile):
    apart = me ^ shard
    n = bits_of(count)
    plain = apart * 0
    turned = apart * 0
    for k in range(n):
        bit = (apart >> k) & 1
        plain = plain | (bit << (n - 1 - k))
        turned = turned | (bit << k)
    return jnp.where(tile == 0, plain, turned)


def exchange(block, axis, count, bits):
    route = []
    for i in range(count):
        for c in range(2):
            route.append((i * 2 + c, (i ^ bits[c]) * 2 + c))
    return lax.ppermute(block, (axis, "tile"), route)


def added(a, b):
    return (a.astype(F32) + b.astype(F32)).astype(BF16)


def passed_along(block, axis, distance):
    count = lax.axis_size(axis)
    route = [(i - distance, i) for i in range(count) if 0 <= i - distance < count]
    return lax.ppermute(block, axis, route)


def swapped(block):
    return lax.ppermute(block, "tile", [(0, 1), (1, 0)])


def body(activations, kernel, conv_bias, cotangent):
    clip_count, frames, height, breadth, channels = activations.shape
    x, upstream = activations[0], cotangent[0]
    tile = lax.axis_index("tile")
    shards = lax.axis_size("dp")
    steps = lax.axis_size("tm")
    share = 27 * channels // shards
    half = -(-(share + 1) // 32) * 16
    arranged = share % 32 == 0

    area = height * breadth
    bias = conv_bias.reshape(1, channels)
    cells = jax.ShapeDtypeStruct(x.shape, BF16)

    def arrays(*shapes, kind=BF16):
        return [jax.ShapeDtypeStruct(shape, kind) for shape in shapes]

    def windows_shape(count):
        return (count, height + 2, breadth, 3 * channels)

    def frames_shape(count):
        return (count, height, breadth, channels)

    def call(kernel_body, name, share, shapes, scratch, far_in, far_out, args, aliases=None):
        here, there = pl.BlockSpec(memory_space=pltpu.VMEM), pl.BlockSpec(memory_space=pltpu.HBM)
        return pl.pallas_call(
            kernel_body,
            out_shape=shapes,
            in_specs=[there if i in far_in else here for i in range(len(args))],
            out_specs=[there if i in far_out else here for i in range(len(shapes))],
            scratch_shapes=scratch,
            input_output_aliases=aliases or {},
            compiler_params=pltpu.CompilerParams(vmem_limit_bytes=32 * 2**20),
            cost_estimate=pl.CostEstimate(
                flops=int(share * 4 * 27 * channels * channels * frames * area),
                bytes_accessed=4 * 2**20,
                transcendentals=0,
            ),
            name=name,
        )(*args)

    dma, vmem = pltpu.SemaphoreType.DMA, pltpu.VMEM
    edge, tail = call(
        border_kernel,
        "border_rows",
        2.0,
        arrays((frames, breadth, channels), frames_shape(2)),
        [dma((2,))],
        (0,),
        (),
        (x,),
    )
    edge = swapped(edge)
    before = passed_along(
        jnp.concatenate(
            [tail.reshape(2 * height, breadth, channels), edge[frames - 2 :]], axis=0
        ),
        "tm",
        1,
    )
    block_out, windows, taps, turned, later_grads, later_edge, total = call(
        interior_kernel,
        "forward_interior",
        0.75,
        [cells]
        + arrays(
            windows_shape(frames),
            (36 * channels, 2 * channels),
            (2 * channels, (frames // 2 - 1) * area),
            frames_shape(frames - 2),
            (frames - 2, breadth, channels),
        )
        + arrays((1, channels), kind=F32),
        [
            vmem((1, channels), F32),
            vmem(frames_shape(frames - 2), BF16),
            vmem(frames_shape(frames - 2), BF16),
            dma((2,)),
            dma((frames // 2 - 1,)),
        ],
        (3, 4),
        (0,),
        (x, edge, kernel, bias, upstream),
    )
    if arranged:
        partial = arrays((2, shards, half, channels))
    else:
        partial = arrays((27, channels, channels)) + arrays((1, channels), kind=F32)
    block_out, early_grads, grad_edge, *parts = call(
        functools.partial(first_frames_kernel, arranged=arranged),
        "first_frames_and_weights",
        1.25,
        [cells] + arrays(frames_shape(2), (frames, breadth, channels)) + partial,
        [
            vmem(windows_shape(2), BF16),
            vmem((1, channels), F32),
            vmem(frames_shape(2), BF16),
            vmem(frames_shape(2), BF16),
            dma((2,)),
            dma,
        ],
        (0, 4, 5),
        (0,),
        (
            block_out,
            x,
            edge,
            before,
            bias,
            upstream,
            windows,
            taps,
            turned,
            later_edge,
            total,
        ),
        {0: 0},
    )
    if arranged:
        kept, sent = parts[0][0], parts[0][1]
    else:
        weight = parts[0].reshape(shards, share, channels)
        line = jnp.broadcast_to(parts[1].astype(BF16)[None], (shards, 1, channels))
        pad = jnp.zeros((shards, 2 * half - share - 1, channels), BF16)
        whole = jnp.concatenate([weight, line, pad], axis=1)
        me = lax.axis_index("dp")
        whole = whole.reshape(shards, 2, half, channels)
        kept, sent = (
            jnp.zeros((shards, half, channels), BF16)
            .at[place_of(me, jnp.arange(shards), shards, side)]
            .set(lax.dynamic_index_in_dim(whole, side, 1, False))
            for side in (tile, 1 - tile)
        )

    total = added(kept, swapped(sent))
    edge = swapped(grad_edge)
    after = passed_along(
        jnp.concatenate(
            [early_grads.reshape(2 * height, breadth, channels), edge[:2]], axis=0
        ),
        "tm",
        -1,
    )
    grad_input, last, taps = call(
        back_interior_kernel,
        "input_gradient_interior",
        0.75,
        [cells] + arrays(windows_shape(2), (2 * channels, 36 * channels)),
        [
            vmem(windows_shape(frames - 2), BF16),
            vmem(frames_shape(frames - 2), BF16),
            vmem(frames_shape(frames - 2), BF16),
            dma,
            dma((frames // 2 - 1,)),
        ],
        (4,),
        (0,),
        (early_grads, later_grads, edge, kernel, upstream),
    )
    n = bits_of(shards)
    for k in range(n):
        if k == n - 1:
            total, grad_input = lax.optimization_barrier((total, grad_input))
        middle = total.shape[0] // 2
        total = added(
            total[:middle], exchange(total[middle:], "dp", shards, (1 << k, 1 << (n - 1 - k)))
        )
    (grad_input,) = call(
        back_last_kernel,
        "input_gradient_last",
        0.25,
        [cells],
        [
            vmem(windows_shape(2), BF16),
            vmem(frames_shape(2), BF16),
            vmem(frames_shape(2), BF16),
            dma,
            dma,
        ],
        (0, 4),
        (0,),
        (grad_input, last, after, taps, upstream),
        {0: 0},
    )
    total = total[0]
    n = bits_of(steps)
    for k in range(n):
        if k == n - 1:
            total, grad_input = lax.optimization_barrier((total, grad_input))
        total = added(total, exchange(total, "tm", steps, (1 << k, 1 << (n - 1 - k))))
    other = swapped(total)
    positions = (
        clip_count * frames * height * breadth * shards * steps * lax.axis_size("tile")
    )
    weight, bias_grad = call(
        functools.partial(closing_kernel, scale=1.0 / math.sqrt(positions)),
        "scaled_weights",
        0.01,
        arrays((share, channels), (1, channels // shards), kind=F32),
        [],
        (),
        (),
        (total, other),
    )
    return block_out[None], grad_input[None], weight, bias_grad.reshape(channels // shards)


def solution(mesh):
    return jax.shard_map(
        body,
        mesh=mesh,
        in_specs=(P("dp", "tm", "tile", None, None), P(), P(), P("dp", "tm", "tile", None, None)),
        out_specs=(
            P("dp", "tm", "tile", None, None),
            P("dp", "tm", "tile", None, None),
            P("dp", None),
            P("dp"),
        ),
        check_vma=False,
    )
```

```python
import functools
import math

import jax
import jax.numpy as jnp
from jax import lax
from jax.experimental import pallas as pl
from jax.experimental.pallas import tpu as pltpu
from jax.sharding import PartitionSpec as P

F32 = jnp.float32
BF16 = jnp.bfloat16


def shifted_columns(cells, breadth):
    count = cells.shape[0]
    wide = cells.astype(F32)
    column = lax.broadcasted_iota(jnp.int32, cells.shape, 0) % breadth
    left = jnp.where(column == 0, 0.0, pltpu.roll(wide, 1, 0))
    right = jnp.where(column == breadth - 1, 0.0, pltpu.roll(wide, count - 1, 0))
    return left.astype(BF16), cells, right.astype(BF16)


def fill_windows(windows, frame, inner, edge, tile):
    height, breadth, channels = inner.shape
    parts = shifted_columns(inner.reshape(height * breadth, channels), breadth)
    edges = shifted_columns(edge, breadth)
    for e in range(3):
        lanes = slice(e * channels, (e + 1) * channels)
        windows[frame, 1 : height + 1, :, lanes] = parts[e].reshape(height, breadth, channels)
        rim = edges[e]
        none = jnp.zeros_like(rim)
        windows[frame, 0, :, lanes] = jnp.where(tile == 0, none, rim)
        windows[frame, height + 1, :, lanes] = jnp.where(tile == 0, rim, none)


def window_block(frames):
    blocks = []
    for frame in frames:
        height = frame.shape[0] - 2
        for b in range(3):
            blocks.append(frame[b : b + height].reshape(-1, frame.shape[-1]))
    return jnp.concatenate(blocks, axis=1)


def activate(pre, source, upstream):
    sigma = jax.nn.sigmoid(pre)
    result = (source.astype(F32) + pre * sigma).astype(BF16)
    grad = (upstream.astype(F32) * sigma * (1.0 + pre * (1.0 - sigma))).astype(BF16)
    return result, grad


def forward_pair(frames, taps, bias, x_pair, upstream):
    channels = bias.shape[1]
    both = jnp.concatenate([bias[...], bias[...]], axis=1)
    pre = both + jnp.dot(window_block(frames), taps[...], preferred_element_type=F32)
    return [
        activate(
            pre[:, s * channels : (s + 1) * channels],
            x_pair[s].reshape(-1, channels),
            upstream[s].reshape(-1, channels),
        )
        for s in range(2)
    ]


def interior_kernel(
    x,
    edge,
    kernel,
    bias,
    cotangent,
    block_out,
    windows,
    taps,
    turned,
    grad_pre,
    edge_out,
    total,
    bias_here,
    upstream,
    result,
    arriving,
    leaving,
):
    frames, height, breadth, channels = x.shape
    area = height * breadth
    tile = lax.axis_index("tile")
    bias_copy = pltpu.make_async_copy(bias, bias_here, arriving.at[0])
    up_copy = pltpu.make_async_copy(cotangent.at[2:frames], upstream, arriving.at[1])
    bias_copy.start()
    up_copy.start()
    rows = 9 * channels
    taps[0 : 3 * rows, 0:channels] = kernel[...]
    taps[3 * rows :, 0:channels] = jnp.zeros((rows, channels), BF16)
    taps[0:rows, channels:] = jnp.zeros((rows, channels), BF16)
    taps[rows:, channels:] = kernel[...]
    @pl.loop(0, frames)
    def _(f):
        fill_windows(windows, f, x[f], edge[f], tile)

    bias_copy.wait()
    up_copy.wait()
    total[...] = jnp.zeros((1, channels), F32)

    def leave(p):
        return pltpu.make_async_copy(
            result.at[pl.ds(2 * p, 2)], block_out.at[pl.ds(2 * p + 2, 2)], leaving
        )

    @pl.loop(0, frames // 2 - 1, unroll=True)
    def _(p):
        outs = forward_pair(
            [windows[2 * p + f] for f in range(4)],
            taps,
            bias_here,
            [x[2 * p + 2], x[2 * p + 3]],
            [upstream[2 * p], upstream[2 * p + 1]],
        )
        summed = jnp.zeros((1, channels), F32)
        for s in range(2):
            t = 2 * p + s
            result[t] = outs[s][0].reshape(height, breadth, channels)
            grad = outs[s][1]
            summed = summed + jnp.sum(grad.astype(F32), axis=0, keepdims=True)
            cube = grad.reshape(height, breadth, channels)
            grad_pre[t] = cube
            edge_out[t] = jnp.where(tile == 0, cube[height - 1], cube[0])
        turned[p] = jnp.concatenate([outs[0][1], outs[1][1]], axis=1).T
        total[...] += summed
        leave(p).start()

    @pl.loop(0, frames // 2 - 1)
    def _(p):
        leave(p).wait()


def first_frames_kernel(
    block_in,
    x,
    edge,
    before,
    bias,
    cotangent,
    windows,
    taps,
    turned,
    edge_in,
    total,
    block_out,
    grad_pre,
    edge_out,
    *rest,
    arranged,
):
    outs, (early, bias_here, upstream, result, arriving, leaving) = rest[:-6], rest[-6:]
    frames, height, breadth, channels = x.shape
    area = height * breadth
    tile = lax.axis_index("tile")
    bias_copy = pltpu.make_async_copy(bias, bias_here, arriving.at[0])
    up_copy = pltpu.make_async_copy(cotangent.at[0:2], upstream, arriving.at[1])
    bias_copy.start()
    up_copy.start()
    for f in range(2):
        fill_windows(early, f, before[f * height : (f + 1) * height], before[2 * height + f], tile)
    bias_copy.wait()
    up_copy.wait()
    summed = total[...]
    firsts = forward_pair(
        [early[0], early[1], windows[0], windows[1]],
        taps,
        bias_here,
        [x[0], x[1]],
        [upstream[0], upstream[1]],
    )
    for s in range(2):
        result[s] = firsts[s][0].reshape(height, breadth, channels)
        cube = firsts[s][1].reshape(height, breadth, channels)
        summed = summed + jnp.sum(firsts[s][1].astype(F32), axis=0, keepdims=True)
        grad_pre[s] = cube
        edge_out[s] = jnp.where(tile == 0, cube[height - 1], cube[0])
    edge_out[2:frames] = edge_in[...]
    copy = pltpu.make_async_copy(result, block_out.at[0:2], leaving)
    copy.start()
    pairs = frames // 2
    pairs = frames // 2
    grads = jnp.concatenate(
        [
            part
            for s in range(2)
            for part in [firsts[s][1].T]
            + [turned[p, s * channels : (s + 1) * channels] for p in range(pairs - 1)]
        ],
        axis=1,
    )

    def tap_row(b, write):
        for a in range(3):
            source = jnp.concatenate(
                [
                    (early if t + a < 2 else windows)[
                        t + a - (0 if t + a < 2 else 2), pl.ds(b, height)
                    ].reshape(area, 3 * channels)
                    for s in range(2)
                    for t in range(s, frames, 2)
                ],
                axis=0,
            )
            product = jnp.dot(grads, source, preferred_element_type=F32).astype(BF16)
            for e in range(3):
                write((a * 3 + b) * 3 + e, product[:, e * channels : (e + 1) * channels].T)

    step = 32
    per_tap = channels // step
    if arranged:
        (parts,) = outs
        count, half = parts.shape[1], parts.shape[2]
        me = lax.axis_index("dp")
        per, per_half = 27 * per_tap // count, half // step
    else:
        weights, bias_sum = outs

    def put(j, at, rows):
        h = at // per_half
        place = place_of(me, j, count, h)
        spot = (at - h * per_half) * step
        if not isinstance(spot, int):
            spot = pl.multiple_of(spot, step)
        parts[tile ^ h, place, pl.ds(spot, step)] = rows

    def tap_rows(b):
        def write(k, block):
            for i in range(per_tap):
                r = k * per_tap + i
                rows = block[i * step : (i + 1) * step]
                if arranged:
                    put(r // per, r % per, rows)
                else:
                    weights[r] = rows

        tap_row(b, write)

    if arranged:
        pl.loop(0, 3)(tap_rows)
    else:
        for b in range(3):
            tap_rows(b)
        bias_sum[...] = summed
        copy.wait()
        return
    line = jnp.concatenate([summed, jnp.zeros((step - 1, channels), F32)], axis=0).astype(BF16)
    for j in range(count):
        put(j, per, line)
    copy.wait()


def back_pair(frames, taps, upstream):
    back = lax.dot_general(
        window_block(frames), taps[...], (((1,), (1,)), ((), ())), preferred_element_type=F32
    )
    channels = back.shape[1] // 2
    return [
        (
            upstream[s].astype(F32)
            + back[:, s * channels : (s + 1) * channels].reshape(upstream[s].shape)
        ).astype(BF16)
        for s in range(2)
    ]


def back_interior_kernel(
    early, g, edge, kernel, cotangent, grad_input, last, taps, windows, upstream, result, arriving, leaving
):
    frames, height, breadth, channels = cotangent.shape
    tile = lax.axis_index("tile")
    up_copy = pltpu.make_async_copy(cotangent.at[0 : frames - 2], upstream, arriving)
    up_copy.start()
    for f in range(4):
        for s in range(2):
            a = 2 - f + s
            for b in range(3):
                for e in range(3):
                    lanes = ((f * 3 + b) * 3 + e) * channels
                    where = (slice(s * channels, (s + 1) * channels), slice(lanes, lanes + channels))
                    if 0 <= a < 3:
                        k = ((a * 3 + 2 - b) * 3 + 2 - e) * channels
                        taps[where] = kernel[k : k + channels]
                    else:
                        taps[where] = jnp.zeros((channels, channels), BF16)
    for f in range(2):
        fill_windows(windows, f, early[f], edge[f], tile)

    @pl.loop(2, frames)
    def _(f):
        fill_windows(windows, f, g[f - 2], edge[f], tile)

    last[...] = windows[frames - 2 : frames]
    up_copy.wait()

    def leave(p):
        return pltpu.make_async_copy(
            result.at[pl.ds(2 * p, 2)], grad_input.at[pl.ds(2 * p, 2)], leaving
        )

    @pl.loop(0, frames // 2 - 1)
    def _(p):
        pair = back_pair(
            [windows[2 * p + f] for f in range(4)],
            taps,
            [upstream[2 * p], upstream[2 * p + 1]],
        )
        for s in range(2):
            result[2 * p + s] = pair[s]
        leave(p).start()

    @pl.loop(0, frames // 2 - 1)
    def _(p):
        leave(p).wait()


def back_last_kernel(
    grad_in, last, after, taps, cotangent, grad_input, windows, upstream, result, arriving, leaving
):
    frames, height, breadth, channels = cotangent.shape
    tile = lax.axis_index("tile")
    up_copy = pltpu.make_async_copy(cotangent.at[frames - 2 : frames], upstream, arriving)
    up_copy.start()
    for f in range(2):
        fill_windows(windows, f, after[f * height : (f + 1) * height], after[2 * height + f], tile)
    up_copy.wait()
    pair = back_pair(
        [last[0], last[1], windows[0], windows[1]], taps, [upstream[0], upstream[1]]
    )
    for s in range(2):
        result[s] = pair[s]
    copy = pltpu.make_async_copy(result, grad_input.at[frames - 2 : frames], leaving)
    copy.start()
    copy.wait()


def border_kernel(x, edge, tail, copied):
    frames, height = x.shape[:2]
    row = jnp.where(lax.axis_index("tile") == 0, height - 1, 0)
    copies = [
        pltpu.make_async_copy(x.at[:, row], edge, copied.at[0]),
        pltpu.make_async_copy(x.at[frames - 2 : frames], tail, copied.at[1]),
    ]
    for copy in copies:
        copy.start()
    for copy in copies:
        copy.wait()


def closing_kernel(own, other, weight, bias, *, scale):
    tile = lax.axis_index("tile")
    half, channels = own.shape
    rest = weight.shape[0] - half
    mine, theirs = own[...].astype(F32) * scale, other[...].astype(F32) * scale
    first = jnp.where(tile == 0, mine, theirs)
    second = jnp.where(tile == 0, theirs, mine)
    weight[0:half] = first
    weight[half:] = second[0:rest]
    line = second[rest : rest + 1]
    share = bias.shape[1]
    spot = lax.axis_index("dp") * share
    picked = jnp.zeros((1, share), F32)
    for j in range(channels // share):
        picked = jnp.where(spot == j * share, line[:, j * share : (j + 1) * share], picked)
    bias[...] = picked


def bits_of(count):
    return count.bit_length() - 1


def place_of(me, shard, count, tile):
    apart = me ^ shard
    n = bits_of(count)
    plain = apart * 0
    turned = apart * 0
    for k in range(n):
        bit = (apart >> k) & 1
        plain = plain | (bit << (n - 1 - k))
        turned = turned | (bit << k)
    return jnp.where(tile == 0, plain, turned)


def exchange(block, axis, count, bits):
    route = []
    for i in range(count):
        for c in range(2):
            route.append((i * 2 + c, (i ^ bits[c]) * 2 + c))
    return lax.ppermute(block, (axis, "tile"), route)


def added(a, b):
    return (a.astype(F32) + b.astype(F32)).astype(BF16)


def passed_along(block, axis, distance):
    count = lax.axis_size(axis)
    route = [(i - distance, i) for i in range(count) if 0 <= i - distance < count]
    return lax.ppermute(block, axis, route)


def swapped(block):
    return lax.ppermute(block, "tile", [(0, 1), (1, 0)])


def body(activations, kernel, conv_bias, cotangent):
    clip_count, frames, height, breadth, channels = activations.shape
    x, upstream = activations[0], cotangent[0]
    tile = lax.axis_index("tile")
    shards = lax.axis_size("dp")
    steps = lax.axis_size("tm")
    share = 27 * channels // shards
    half = -(-(share + 1) // 32) * 16
    arranged = share % 32 == 0

    area = height * breadth
    bias = conv_bias.reshape(1, channels)
    cells = jax.ShapeDtypeStruct(x.shape, BF16)

    def arrays(*shapes, kind=BF16):
        return [jax.ShapeDtypeStruct(shape, kind) for shape in shapes]

    def windows_shape(count):
        return (count, height + 2, breadth, 3 * channels)

    def frames_shape(count):
        return (count, height, breadth, channels)

    def call(kernel_body, name, share, shapes, scratch, far_in, far_out, args, aliases=None):
        here, there = pl.BlockSpec(memory_space=pltpu.VMEM), pl.BlockSpec(memory_space=pltpu.HBM)
        return pl.pallas_call(
            kernel_body,
            out_shape=shapes,
            in_specs=[there if i in far_in else here for i in range(len(args))],
            out_specs=[there if i in far_out else here for i in range(len(shapes))],
            scratch_shapes=scratch,
            input_output_aliases=aliases or {},
            compiler_params=pltpu.CompilerParams(vmem_limit_bytes=32 * 2**20),
            cost_estimate=pl.CostEstimate(
                flops=int(share * 4 * 27 * channels * channels * frames * area),
                bytes_accessed=4 * 2**20,
                transcendentals=0,
            ),
            name=name,
        )(*args)

    dma, vmem = pltpu.SemaphoreType.DMA, pltpu.VMEM
    edge, tail = call(
        border_kernel,
        "border_rows",
        2.0,
        arrays((frames, breadth, channels), frames_shape(2)),
        [dma((2,))],
        (0,),
        (),
        (x,),
    )
    edge = swapped(edge)
    before = passed_along(
        jnp.concatenate(
            [tail.reshape(2 * height, breadth, channels), edge[frames - 2 :]], axis=0
        ),
        "tm",
        1,
    )
    block_out, windows, taps, turned, later_grads, later_edge, total = call(
        interior_kernel,
        "forward_interior",
        0.75,
        [cells]
        + arrays(
            windows_shape(frames),
            (36 * channels, 2 * channels),
            (frames // 2 - 1, 2 * channels, area),
            frames_shape(frames - 2),
            (frames - 2, breadth, channels),
        )
        + arrays((1, channels), kind=F32),
        [
            vmem((1, channels), F32),
            vmem(frames_shape(frames - 2), BF16),
            vmem(frames_shape(frames - 2), BF16),
            dma((2,)),
            dma,
        ],
        (3, 4),
        (0,),
        (x, edge, kernel, bias, upstream),
    )
    if arranged:
        partial = arrays((2, shards, half, channels))
    else:
        partial = arrays((27 * channels // 32, 32, channels)) + arrays((1, channels), kind=F32)
    block_out, early_grads, grad_edge, *parts = call(
        functools.partial(first_frames_kernel, arranged=arranged),
        "first_frames_and_weights",
        1.25,
        [cells] + arrays(frames_shape(2), (frames, breadth, channels)) + partial,
        [
            vmem(windows_shape(2), BF16),
            vmem((1, channels), F32),
            vmem(frames_shape(2), BF16),
            vmem(frames_shape(2), BF16),
            dma((2,)),
            dma,
        ],
        (0, 4, 5),
        (0,),
        (
            block_out,
            x,
            edge,
            before,
            bias,
            upstream,
            windows,
            taps,
            turned,
            later_edge,
            total,
        ),
        {0: 0},
    )
    if arranged:
        kept, sent = parts[0][0], parts[0][1]
    else:
        weight = parts[0].reshape(shards, share, channels)
        line = jnp.broadcast_to(parts[1].astype(BF16)[None], (shards, 1, channels))
        pad = jnp.zeros((shards, 2 * half - share - 1, channels), BF16)
        whole = jnp.concatenate([weight, line, pad], axis=1)
        me = lax.axis_index("dp")
        whole = whole.reshape(shards, 2, half, channels)
        kept, sent = (
            jnp.zeros((shards, half, channels), BF16)
            .at[place_of(me, jnp.arange(shards), shards, side)]
            .set(lax.dynamic_index_in_dim(whole, side, 1, False))
            for side in (tile, 1 - tile)
        )

    total = added(kept, swapped(sent))
    edge = swapped(grad_edge)
    edge, total = lax.optimization_barrier((edge, total))
    grad_input, last, taps = call(
        back_interior_kernel,
        "input_gradient_interior",
        0.75,
        [cells] + arrays(windows_shape(2), (2 * channels, 36 * channels)),
        [
            vmem(windows_shape(frames), BF16),
            vmem(frames_shape(frames - 2), BF16),
            vmem(frames_shape(frames - 2), BF16),
            dma,
            dma,
        ],
        (4,),
        (0,),
        (early_grads, later_grads, edge, kernel, upstream),
    )
    first_edge, last = lax.optimization_barrier((edge[:2], last))
    after = passed_along(
        jnp.concatenate(
            [early_grads.reshape(2 * height, breadth, channels), first_edge], axis=0
        ),
        "tm",
        -1,
    )
    if shards == 4:
        apart = {1: (2, 1), 2: (1, 2), 3: (3, 3)}
        parts = [exchange(total[k], "dp", shards, apart[k]) for k in (3, 1, 2)]
        total = total[0].astype(F32)
        for part in parts:
            total = total + part.astype(F32)
        total = total.astype(BF16)
    else:
        n = bits_of(shards)
        for k in range(n):
            middle = total.shape[0] // 2
            total = added(
                total[:middle], exchange(total[middle:], "dp", shards, (1 << k, 1 << (n - 1 - k)))
            )
        total = total[0]
    total, grad_input = lax.optimization_barrier((total, grad_input))
    (grad_input,) = call(
        back_last_kernel,
        "input_gradient_last",
        0.25,
        [cells],
        [
            vmem(windows_shape(2), BF16),
            vmem(frames_shape(2), BF16),
            vmem(frames_shape(2), BF16),
            dma,
            dma,
        ],
        (0, 4),
        (0,),
        (grad_input, last, after, taps, upstream),
        {0: 0},
    )
    got = {k: exchange(total, "tm", steps, (k, k if k == 3 else 3 - k)) for k in (3, 2, 1)}
    total = (
        (total.astype(F32) + got[1].astype(F32)) + (got[2].astype(F32) + got[3].astype(F32))
    ).astype(BF16)
    total, grad_input = lax.optimization_barrier((total, grad_input))
    other = swapped(total)
    positions = (
        clip_count * frames * height * breadth * shards * steps * lax.axis_size("tile")
    )
    weight, bias_grad = call(
        functools.partial(closing_kernel, scale=1.0 / math.sqrt(positions)),
        "scaled_weights",
        0.01,
        arrays((share, channels), (1, channels // shards), kind=F32),
        [],
        (),
        (),
        (total, other),
    )
    return block_out[None], grad_input[None], weight, bias_grad.reshape(channels // shards)


def solution(mesh):
    return jax.shard_map(
        body,
        mesh=mesh,
        in_specs=(P("dp", "tm", "tile", None, None), P(), P(), P("dp", "tm", "tile", None, None)),
        out_specs=(
            P("dp", "tm", "tile", None, None),
            P("dp", "tm", "tile", None, None),
            P("dp", None),
            P("dp"),
        ),
        check_vma=False,
    )
```

```python
import functools
import math

import jax
import jax.numpy as jnp
from jax import lax
from jax.experimental import pallas as pl
from jax.experimental.pallas import tpu as pltpu
from jax.sharding import PartitionSpec as P

F32 = jnp.float32
BF16 = jnp.bfloat16


def shifted_columns(cells, breadth):
    count = cells.shape[0]
    wide = cells.astype(F32)
    column = lax.broadcasted_iota(jnp.int32, cells.shape, 0) % breadth
    left = jnp.where(column == 0, 0.0, pltpu.roll(wide, 1, 0))
    right = jnp.where(column == breadth - 1, 0.0, pltpu.roll(wide, count - 1, 0))
    return left.astype(BF16), cells, right.astype(BF16)


def fill_windows(windows, frame, inner, edge, tile):
    height, breadth, channels = inner.shape
    parts = shifted_columns(inner.reshape(height * breadth, channels), breadth)
    edges = shifted_columns(edge, breadth)
    for e in range(3):
        lanes = slice(e * channels, (e + 1) * channels)
        windows[frame, 1 : height + 1, :, lanes] = parts[e].reshape(height, breadth, channels)
        rim = edges[e]
        none = jnp.zeros_like(rim)
        windows[frame, 0, :, lanes] = jnp.where(tile == 0, none, rim)
        windows[frame, height + 1, :, lanes] = jnp.where(tile == 0, rim, none)


def window_block(frames):
    blocks = []
    for frame in frames:
        height = frame.shape[0] - 2
        for b in range(3):
            blocks.append(frame[b : b + height].reshape(-1, frame.shape[-1]))
    return jnp.concatenate(blocks, axis=1)


def activate(pre, source, upstream):
    sigma = jax.nn.sigmoid(pre)
    result = (source.astype(F32) + pre * sigma).astype(BF16)
    grad = (upstream.astype(F32) * sigma * (1.0 + pre * (1.0 - sigma))).astype(BF16)
    return result, grad


def forward_pair(frames, taps, bias, x_pair, upstream):
    channels = bias.shape[1]
    both = jnp.concatenate([bias[...], bias[...]], axis=1)
    pre = both + jnp.dot(window_block(frames), taps[...], preferred_element_type=F32)
    return [
        activate(
            pre[:, s * channels : (s + 1) * channels],
            x_pair[s].reshape(-1, channels),
            upstream[s].reshape(-1, channels),
        )
        for s in range(2)
    ]


def interior_kernel(
    x,
    edge,
    kernel,
    bias,
    cotangent,
    block_out,
    windows,
    taps,
    turned,
    grad_pre,
    edge_out,
    total,
    bias_here,
    upstream,
    result,
    arriving,
    leaving,
):
    frames, height, breadth, channels = x.shape
    area = height * breadth
    tile = lax.axis_index("tile")
    bias_copy = pltpu.make_async_copy(bias, bias_here, arriving.at[0])
    up_copy = pltpu.make_async_copy(cotangent.at[2:frames], upstream, arriving.at[1])
    bias_copy.start()
    up_copy.start()
    rows = 9 * channels
    taps[0 : 3 * rows, 0:channels] = kernel[...]
    taps[3 * rows :, 0:channels] = jnp.zeros((rows, channels), BF16)
    taps[0:rows, channels:] = jnp.zeros((rows, channels), BF16)
    taps[rows:, channels:] = kernel[...]
    @pl.loop(0, frames)
    def _(f):
        fill_windows(windows, f, x[f], edge[f], tile)

    bias_copy.wait()
    up_copy.wait()
    total[...] = jnp.zeros((1, channels), F32)

    def leave(p):
        return pltpu.make_async_copy(
            result.at[pl.ds(2 * p, 2)], block_out.at[pl.ds(2 * p + 2, 2)], leaving
        )

    @pl.loop(0, frames // 2 - 1, unroll=True)
    def _(p):
        outs = forward_pair(
            [windows[2 * p + f] for f in range(4)],
            taps,
            bias_here,
            [x[2 * p + 2], x[2 * p + 3]],
            [upstream[2 * p], upstream[2 * p + 1]],
        )
        summed = jnp.zeros((1, channels), F32)
        for s in range(2):
            t = 2 * p + s
            result[t] = outs[s][0].reshape(height, breadth, channels)
            grad = outs[s][1]
            summed = summed + jnp.sum(grad.astype(F32), axis=0, keepdims=True)
            cube = grad.reshape(height, breadth, channels)
            grad_pre[t] = cube
            edge_out[t] = jnp.where(tile == 0, cube[height - 1], cube[0])
        turned[p] = jnp.concatenate([outs[0][1], outs[1][1]], axis=1).T
        total[...] += summed
        leave(p).start()

    @pl.loop(0, frames // 2 - 1)
    def _(p):
        leave(p).wait()


STEP = 32
GROUP = 12
HALVES = (
    (
        (*range(0, 12), 24, 25),
        (*range(36, 48), 27, 28),
        (*range(60, 74),),
        (*range(84, 96), 81, 82),
    ),
    (
        (*range(12, 24), 26),
        (*range(29, 36), *range(48, 54)),
        (*range(54, 60), *range(74, 81)),
        (*range(96, 108), 83),
    ),
)
LEAVING = (0x866421, 0x765320)
STAYING = (0x7530, 0x8841)
COUNTS = {LEAVING: (6, 3), STAYING: (4, 4)}


def runs_of(steps):
    runs = []
    for position, step in enumerate(steps):
        if runs and step == runs[-1][1] + runs[-1][2] and step % GROUP:
            runs[-1][2] += 1
        else:
            runs.append([position, step, 1])
    return runs


def place_half(target, half, blocks, total, me):
    for j, steps in enumerate(HALVES[half]):
        spot = me ^ j
        for position, step, count in runs_of(steps):
            g, at = step // GROUP, step % GROUP * STEP
            target[spot, position * STEP : (position + count) * STEP] = blocks(
                g, at, at + count * STEP
            )
        if half == 1:
            line = jnp.concatenate(
                [total, jnp.zeros((STEP - 1, total.shape[1]), F32)], axis=0
            ).astype(BF16)
            target[spot, len(steps) * STEP : (len(steps) + 1) * STEP] = line


def group_loop(codes, front, windows, grads, blocks, tile):
    channels = grads.shape[0]
    frames = windows.shape[0]
    height = windows.shape[1] - 2
    code = jnp.where(tile == 0, codes[0], codes[1])
    count, together = COUNTS[codes]

    @pl.loop(0, count // together)
    def _(i):
        for k in range(together):
            g = lax.shift_right_logical(code, 4 * (together * i + k)) & 15
            a, b = g // 3, g % 3
            source = jnp.concatenate(
                [
                    (
                        front[t + a, pl.ds(b, height)]
                        if t < 2
                        else windows[t - 2 + a, pl.ds(b, height)]
                    ).reshape(-1, 3 * channels)
                    for s in range(2)
                    for t in range(s, frames, 2)
                ],
                axis=0,
            )
            product = jnp.dot(grads[...], source, preferred_element_type=F32).astype(BF16)
            for e in range(3):
                lanes = slice(e * channels, (e + 1) * channels)
                blocks[g, lanes] = product[:, lanes].T


def first_frames(
    x, before, bias, cotangent, windows, taps, turned, edge_in, total, block_out, grad_pre, edge_out,
    early, bias_here, upstream, result, arriving, leaving,
):
    frames, height, breadth, channels = x.shape
    tile = lax.axis_index("tile")
    bias_copy = pltpu.make_async_copy(bias, bias_here, arriving.at[0])
    up_copy = pltpu.make_async_copy(cotangent.at[0:2], upstream, arriving.at[1])
    bias_copy.start()
    up_copy.start()
    for f in range(2):
        fill_windows(early, f, before[f * height : (f + 1) * height], before[2 * height + f], tile)
    bias_copy.wait()
    up_copy.wait()
    summed = total[...]
    firsts = forward_pair(
        [early[0], early[1], windows[0], windows[1]],
        taps,
        bias_here,
        [x[0], x[1]],
        [upstream[0], upstream[1]],
    )
    for s in range(2):
        result[s] = firsts[s][0].reshape(height, breadth, channels)
        cube = firsts[s][1].reshape(height, breadth, channels)
        summed = summed + jnp.sum(firsts[s][1].astype(F32), axis=0, keepdims=True)
        grad_pre[s] = cube
        edge_out[s] = jnp.where(tile == 0, cube[height - 1], cube[0])
    edge_out[2:frames] = edge_in[...]
    copy = pltpu.make_async_copy(result, block_out.at[0:2], leaving)
    copy.start()
    grads = jnp.concatenate(
        [
            part
            for s in range(2)
            for part in [firsts[s][1].T]
            + [turned[p, s * channels : (s + 1) * channels] for p in range(frames // 2 - 1)]
        ],
        axis=1,
    )
    return grads, summed, copy


def leaving_half_kernel(
    block_in, x, before, bias, cotangent, windows, taps, turned, edge_in, total,
    block_out, grad_pre, edge_out, sent, blocks, front, grads, total_out,
    bias_here, upstream, result, arriving, leaving,
):
    tile = lax.axis_index("tile")
    me = lax.axis_index("dp")
    front[2:4] = windows[0:2]
    values, summed, copy = first_frames(
        x, before, bias, cotangent, windows, taps, turned, edge_in, total, block_out, grad_pre, edge_out,
        front, bias_here, upstream, result, arriving, leaving,
    )
    grads[...] = values
    total_out[...] = summed
    group_loop(LEAVING, front, windows, grads, blocks, tile)
    for own in range(2):

        @pl.when(tile == own)
        def _():
            place_half(sent, 1 - own, lambda g, low, high: blocks[g, low:high], summed, me)

    copy.wait()


def staying_half_kernel(blocks_in, front, windows, grads, total, kept, blocks):
    tile = lax.axis_index("tile")
    me = lax.axis_index("dp")
    group_loop(STAYING, front, windows, grads, blocks, tile)
    for own in range(2):
        mine = [STAYING[own] >> 4 * i & 15 for i in range(COUNTS[STAYING][0])]

        @pl.when(tile == own)
        def _():
            place_half(
                kept,
                own,
                lambda g, low, high: (blocks if g in mine else blocks_in)[g, low:high],
                total[...],
                me,
            )


def whole_weights_kernel(
    block_in, x, before, bias, cotangent, windows, taps, turned, edge_in, total,
    block_out, grad_pre, edge_out, weights, bias_sum,
    early, bias_here, upstream, result, arriving, leaving,
):
    frames, height, breadth, channels = x.shape
    grads, summed, copy = first_frames(
        x, before, bias, cotangent, windows, taps, turned, edge_in, total, block_out, grad_pre, edge_out,
        early, bias_here, upstream, result, arriving, leaving,
    )
    for b in range(3):
        for a in range(3):
            source = jnp.concatenate(
                [
                    (early[t + a, b : b + height] if t + a < 2 else windows[t + a - 2, b : b + height])
                    .reshape(-1, 3 * channels)
                    for s in range(2)
                    for t in range(s, frames, 2)
                ],
                axis=0,
            )
            product = jnp.dot(grads, source, preferred_element_type=F32).astype(BF16)
            for e in range(3):
                weights[(a * 3 + b) * 3 + e] = product[:, e * channels : (e + 1) * channels].T
    bias_sum[...] = summed
    copy.wait()


def back_pair(frames, taps, upstream):
    back = lax.dot_general(
        window_block(frames), taps[...], (((1,), (1,)), ((), ())), preferred_element_type=F32
    )
    channels = back.shape[1] // 2
    return [
        (
            upstream[s].astype(F32)
            + back[:, s * channels : (s + 1) * channels].reshape(upstream[s].shape)
        ).astype(BF16)
        for s in range(2)
    ]


def back_interior_kernel(
    early, g, edge, kernel, cotangent, grad_input, last, taps, windows, upstream, result, arriving, leaving
):
    frames, height, breadth, channels = cotangent.shape
    tile = lax.axis_index("tile")
    up_copy = pltpu.make_async_copy(cotangent.at[0 : frames - 2], upstream, arriving)
    up_copy.start()
    for f in range(4):
        for s in range(2):
            a = 2 - f + s
            for b in range(3):
                for e in range(3):
                    lanes = ((f * 3 + b) * 3 + e) * channels
                    where = (slice(s * channels, (s + 1) * channels), slice(lanes, lanes + channels))
                    if 0 <= a < 3:
                        k = ((a * 3 + 2 - b) * 3 + 2 - e) * channels
                        taps[where] = kernel[k : k + channels]
                    else:
                        taps[where] = jnp.zeros((channels, channels), BF16)
    for f in range(2):
        fill_windows(windows, f, early[f], edge[f], tile)

    @pl.loop(2, frames)
    def _(f):
        fill_windows(windows, f, g[f - 2], edge[f], tile)

    last[...] = windows[frames - 2 : frames]
    up_copy.wait()

    def leave(p):
        return pltpu.make_async_copy(
            result.at[pl.ds(2 * p, 2)], grad_input.at[pl.ds(2 * p, 2)], leaving
        )

    @pl.loop(0, frames // 2 - 1)
    def _(p):
        pair = back_pair(
            [windows[2 * p + f] for f in range(4)],
            taps,
            [upstream[2 * p], upstream[2 * p + 1]],
        )
        for s in range(2):
            result[2 * p + s] = pair[s]
        leave(p).start()

    @pl.loop(0, frames // 2 - 1)
    def _(p):
        leave(p).wait()


def back_last_kernel(
    grad_in, last, after, taps, cotangent, grad_input, windows, upstream, result, arriving, leaving
):
    frames, height, breadth, channels = cotangent.shape
    tile = lax.axis_index("tile")
    up_copy = pltpu.make_async_copy(cotangent.at[frames - 2 : frames], upstream, arriving)
    up_copy.start()
    for f in range(2):
        fill_windows(windows, f, after[f * height : (f + 1) * height], after[2 * height + f], tile)
    up_copy.wait()
    pair = back_pair(
        [last[0], last[1], windows[0], windows[1]], taps, [upstream[0], upstream[1]]
    )
    for s in range(2):
        result[s] = pair[s]
    copy = pltpu.make_async_copy(result, grad_input.at[frames - 2 : frames], leaving)
    copy.start()
    copy.wait()


def border_kernel(x, edge, tail, copied):
    frames, height = x.shape[:2]
    row = jnp.where(lax.axis_index("tile") == 0, height - 1, 0)
    copies = [
        pltpu.make_async_copy(x.at[:, row], edge, copied.at[0]),
        pltpu.make_async_copy(x.at[frames - 2 : frames], tail, copied.at[1]),
    ]
    for copy in copies:
        copy.start()
    for copy in copies:
        copy.wait()


def closing_kernel(own, other, weight, bias, *, scale, arranged):
    tile = lax.axis_index("tile")
    me = lax.axis_index("dp")
    half, channels = own.shape
    mine, theirs = own[...].astype(F32) * scale, other[...].astype(F32) * scale
    halves = jnp.where(tile == 0, mine, theirs), jnp.where(tile == 0, theirs, mine)
    if arranged:
        per = weight.shape[0] // STEP
        at = (len(HALVES[1][0]) * STEP) % half
        for j in range(len(HALVES[0])):

            @pl.when(me == j)
            def _():
                for h in range(2):
                    for position, step, count in runs_of(HALVES[h][j]):
                        q = (step - j * per) * STEP
                        weight[q : q + count * STEP] = halves[h][
                            position * STEP : (position + count) * STEP
                        ]

    else:
        at = weight.shape[0] - half
        weight[0:half] = halves[0]
        weight[half:] = halves[1][0:at]
    line = halves[1][at : at + 1]
    share = bias.shape[1]
    picked = jnp.zeros((1, share), F32)
    for j in range(channels // share):
        picked = jnp.where(me == j, line[:, j * share : (j + 1) * share], picked)
    bias[...] = picked


def bits_of(count):
    return count.bit_length() - 1


def place_of(me, shard, count, tile):
    apart = me ^ shard
    n = bits_of(count)
    plain = apart * 0
    turned = apart * 0
    for k in range(n):
        bit = (apart >> k) & 1
        plain = plain | (bit << (n - 1 - k))
        turned = turned | (bit << k)
    return jnp.where(tile == 0, plain, turned)


def exchange(block, axis, count, bits):
    route = []
    for i in range(count):
        for c in range(2):
            route.append((i * 2 + c, (i ^ bits[c]) * 2 + c))
    return lax.ppermute(block, (axis, "tile"), route)


def added(a, b):
    return (a.astype(F32) + b.astype(F32)).astype(BF16)


def passed_along(block, axis, distance):
    count = lax.axis_size(axis)
    route = [(i - distance, i) for i in range(count) if 0 <= i - distance < count]
    return lax.ppermute(block, axis, route)


def swapped(block):
    return lax.ppermute(block, "tile", [(0, 1), (1, 0)])


def body(activations, kernel, conv_bias, cotangent):
    clip_count, frames, height, breadth, channels = activations.shape
    x, upstream = activations[0], cotangent[0]
    tile = lax.axis_index("tile")
    shards = lax.axis_size("dp")
    steps = lax.axis_size("tm")
    share = 27 * channels // shards
    half = -(-(share + 1) // 32) * 16
    arranged = shards == 4 and channels == 128

    area = height * breadth
    bias = conv_bias.reshape(1, channels)
    cells = jax.ShapeDtypeStruct(x.shape, BF16)

    def arrays(*shapes, kind=BF16):
        return [jax.ShapeDtypeStruct(shape, kind) for shape in shapes]

    def windows_shape(count):
        return (count, height + 2, breadth, 3 * channels)

    def frames_shape(count):
        return (count, height, breadth, channels)

    def call(kernel_body, name, share, shapes, scratch, far_in, far_out, args, aliases=None):
        here, there = pl.BlockSpec(memory_space=pltpu.VMEM), pl.BlockSpec(memory_space=pltpu.HBM)
        return pl.pallas_call(
            kernel_body,
            out_shape=shapes,
            in_specs=[there if i in far_in else here for i in range(len(args))],
            out_specs=[there if i in far_out else here for i in range(len(shapes))],
            scratch_shapes=scratch,
            input_output_aliases=aliases or {},
            compiler_params=pltpu.CompilerParams(vmem_limit_bytes=32 * 2**20),
            cost_estimate=pl.CostEstimate(
                flops=int(share * 4 * 27 * channels * channels * frames * area),
                bytes_accessed=4 * 2**20,
                transcendentals=0,
            ),
            name=name,
        )(*args)

    dma, vmem = pltpu.SemaphoreType.DMA, pltpu.VMEM
    edge, tail = call(
        border_kernel,
        "border_rows",
        2.0,
        arrays((frames, breadth, channels), frames_shape(2)),
        [dma((2,))],
        (0,),
        (),
        (x,),
    )
    edge = swapped(edge)
    before = passed_along(
        jnp.concatenate(
            [tail.reshape(2 * height, breadth, channels), edge[frames - 2 :]], axis=0
        ),
        "tm",
        1,
    )
    block_out, windows, taps, turned, later_grads, later_edge, total = call(
        interior_kernel,
        "forward_interior",
        0.75,
        [cells]
        + arrays(
            windows_shape(frames),
            (36 * channels, 2 * channels),
            (frames // 2 - 1, 2 * channels, area),
            frames_shape(frames - 2),
            (frames - 2, breadth, channels),
        )
        + arrays((1, channels), kind=F32),
        [
            vmem((1, channels), F32),
            vmem(frames_shape(frames - 2), BF16),
            vmem(frames_shape(frames - 2), BF16),
            dma((2,)),
            dma,
        ],
        (3, 4),
        (0,),
        (x, edge, kernel, bias, upstream),
    )
    front_scratch = [
        vmem((1, channels), F32),
        vmem(frames_shape(2), BF16),
        vmem(frames_shape(2), BF16),
        dma((2,)),
        dma,
    ]
    firsts = [cells] + arrays(frames_shape(2), (frames, breadth, channels))
    operands = (
        block_out, x, before, bias, upstream, windows, taps, turned, later_edge, total,
    )
    if arranged:
        groups = arrays((9, 3 * channels, channels))
        block_out, early_grads, grad_edge, sent, blocks, front, grads, total = call(
            leaving_half_kernel,
            "first_frames_and_leaving_half",
            0.8,
            firsts
            + arrays((shards, half, channels))
            + groups
            + arrays(windows_shape(4), (channels, frames * area))
            + arrays((1, channels), kind=F32),
            front_scratch,
            (0, 3, 4),
            (0,),
            operands,
            {0: 0},
        )
        (kept,) = call(
            staying_half_kernel,
            "staying_half",
            0.45,
            arrays((shards, half, channels)),
            [vmem((9, 3 * channels, channels), BF16)],
            (),
            (),
            (blocks, front, windows, grads, total),
        )
    else:
        block_out, early_grads, grad_edge, weight, line = call(
            whole_weights_kernel,
            "first_frames_and_weights",
            1.25,
            firsts + arrays((27, channels, channels)) + arrays((1, channels), kind=F32),
            [vmem(windows_shape(2), BF16)] + front_scratch,
            (0, 3, 4),
            (0,),
            operands,
            {0: 0},
        )
        weight = weight.reshape(shards, share, channels)
        line = jnp.broadcast_to(line.astype(BF16)[None], (shards, 1, channels))
        pad = jnp.zeros((shards, 2 * half - share - 1, channels), BF16)
        whole = jnp.concatenate([weight, line, pad], axis=1)
        me = lax.axis_index("dp")
        whole = whole.reshape(shards, 2, half, channels)
        kept, sent = (
            jnp.zeros((shards, half, channels), BF16)
            .at[place_of(me, jnp.arange(shards), shards, side)]
            .set(lax.dynamic_index_in_dim(whole, side, 1, False))
            for side in (tile, 1 - tile)
        )

    total = added(kept, swapped(sent))
    edge = swapped(grad_edge)
    edge, total = lax.optimization_barrier((edge, total))
    grad_input, last, taps = call(
        back_interior_kernel,
        "input_gradient_interior",
        0.75,
        [cells] + arrays(windows_shape(2), (2 * channels, 36 * channels)),
        [
            vmem(windows_shape(frames), BF16),
            vmem(frames_shape(frames - 2), BF16),
            vmem(frames_shape(frames - 2), BF16),
            dma,
            dma,
        ],
        (4,),
        (0,),
        (early_grads, later_grads, edge, kernel, upstream),
    )
    first_edge, last = lax.optimization_barrier((edge[:2], last))
    after = passed_along(
        jnp.concatenate(
            [early_grads.reshape(2 * height, breadth, channels), first_edge], axis=0
        ),
        "tm",
        -1,
    )
    if arranged:
        parts = [exchange(total[k], "dp", shards, (k, k)) for k in (3, 1, 2)]
        total = total[0].astype(F32)
        for part in parts:
            total = total + part.astype(F32)
        total = total.astype(BF16)
    else:
        n = bits_of(shards)
        for k in range(n):
            middle = total.shape[0] // 2
            total = added(
                total[:middle], exchange(total[middle:], "dp", shards, (1 << k, 1 << (n - 1 - k)))
            )
        total = total[0]
    total, grad_input = lax.optimization_barrier((total, grad_input))
    (grad_input,) = call(
        back_last_kernel,
        "input_gradient_last",
        0.25,
        [cells],
        [
            vmem(windows_shape(2), BF16),
            vmem(frames_shape(2), BF16),
            vmem(frames_shape(2), BF16),
            dma,
            dma,
        ],
        (0, 4),
        (0,),
        (grad_input, last, after, taps, upstream),
        {0: 0},
    )
    got = {k: exchange(total, "tm", steps, (k, k if k == 3 else 3 - k)) for k in (3, 2, 1)}
    total = (
        (total.astype(F32) + got[1].astype(F32)) + (got[2].astype(F32) + got[3].astype(F32))
    ).astype(BF16)
    total, grad_input = lax.optimization_barrier((total, grad_input))
    other = swapped(total)
    positions = (
        clip_count * frames * height * breadth * shards * steps * lax.axis_size("tile")
    )
    weight, bias_grad = call(
        functools.partial(closing_kernel, scale=1.0 / math.sqrt(positions), arranged=arranged),
        "scaled_weights",
        0.01,
        arrays((share, channels), (1, channels // shards), kind=F32),
        [],
        (),
        (),
        (total, other),
    )
    return block_out[None], grad_input[None], weight, bias_grad.reshape(channels // shards)


def solution(mesh):
    return jax.shard_map(
        body,
        mesh=mesh,
        in_specs=(P("dp", "tm", "tile", None, None), P(), P(), P("dp", "tm", "tile", None, None)),
        out_specs=(
            P("dp", "tm", "tile", None, None),
            P("dp", "tm", "tile", None, None),
            P("dp", None),
            P("dp"),
        ),
        check_vma=False,
    )
```

```python
import functools
import math

import jax
import jax.numpy as jnp
from jax import lax
from jax.experimental import pallas as pl
from jax.experimental.pallas import tpu as pltpu
from jax.sharding import PartitionSpec as P

F32 = jnp.float32
BF16 = jnp.bfloat16


def shifted_columns(cells, breadth):
    count = cells.shape[0]
    wide = cells.astype(F32)
    column = lax.broadcasted_iota(jnp.int32, cells.shape, 0) % breadth
    left = jnp.where(column == 0, 0.0, pltpu.roll(wide, 1, 0))
    right = jnp.where(column == breadth - 1, 0.0, pltpu.roll(wide, count - 1, 0))
    return left.astype(BF16), cells, right.astype(BF16)


def fill_windows(windows, frame, inner, edge, tile):
    height, breadth, channels = inner.shape
    parts = shifted_columns(inner.reshape(height * breadth, channels), breadth)
    edges = shifted_columns(edge, breadth)
    for e in range(3):
        lanes = slice(e * channels, (e + 1) * channels)
        windows[frame, 1 : height + 1, :, lanes] = parts[e].reshape(height, breadth, channels)
        rim = edges[e]
        none = jnp.zeros_like(rim)
        windows[frame, 0, :, lanes] = jnp.where(tile == 0, none, rim)
        windows[frame, height + 1, :, lanes] = jnp.where(tile == 0, rim, none)


def window_block(frames):
    blocks = []
    for frame in frames:
        height = frame.shape[0] - 2
        for b in range(3):
            blocks.append(frame[b : b + height].reshape(-1, frame.shape[-1]))
    return jnp.concatenate(blocks, axis=1)


def activate(pre, source, upstream):
    sigma = jax.nn.sigmoid(pre)
    result = (source.astype(F32) + pre * sigma).astype(BF16)
    grad = (upstream.astype(F32) * sigma * (1.0 + pre * (1.0 - sigma))).astype(BF16)
    return result, grad


def forward_pair(frames, taps, bias, x_pair, upstream):
    channels = bias.shape[1]
    both = jnp.concatenate([bias[...], bias[...]], axis=1)
    pre = both + jnp.dot(window_block(frames), taps[...], preferred_element_type=F32)
    return [
        activate(
            pre[:, s * channels : (s + 1) * channels],
            x_pair[s].reshape(-1, channels),
            upstream[s].reshape(-1, channels),
        )
        for s in range(2)
    ]


def interior_kernel(
    x,
    edge,
    kernel,
    bias,
    cotangent,
    block_out,
    windows,
    taps,
    turned,
    grad_pre,
    edge_out,
    total,
    bias_here,
    upstream,
    result,
    arriving,
    leaving,
):
    frames, height, breadth, channels = x.shape
    area = height * breadth
    tile = lax.axis_index("tile")
    bias_copy = pltpu.make_async_copy(bias, bias_here, arriving.at[0])
    up_copy = pltpu.make_async_copy(cotangent.at[2:frames], upstream, arriving.at[1])
    bias_copy.start()
    up_copy.start()
    rows = 9 * channels
    taps[0 : 3 * rows, 0:channels] = kernel[...]
    taps[3 * rows :, 0:channels] = jnp.zeros((rows, channels), BF16)
    taps[0:rows, channels:] = jnp.zeros((rows, channels), BF16)
    taps[rows:, channels:] = kernel[...]
    @pl.loop(0, frames)
    def _(f):
        fill_windows(windows, f, x[f], edge[f], tile)

    bias_copy.wait()
    up_copy.wait()
    total[...] = jnp.zeros((1, channels), F32)

    def leave(p):
        return pltpu.make_async_copy(
            result.at[pl.ds(2 * p, 2)], block_out.at[pl.ds(2 * p + 2, 2)], leaving
        )

    @pl.loop(0, frames // 2 - 1, unroll=True)
    def _(p):
        outs = forward_pair(
            [windows[2 * p + f] for f in range(4)],
            taps,
            bias_here,
            [x[2 * p + 2], x[2 * p + 3]],
            [upstream[2 * p], upstream[2 * p + 1]],
        )
        summed = jnp.zeros((1, channels), F32)
        for s in range(2):
            t = 2 * p + s
            result[t] = outs[s][0].reshape(height, breadth, channels)
            grad = outs[s][1]
            summed = summed + jnp.sum(grad.astype(F32), axis=0, keepdims=True)
            cube = grad.reshape(height, breadth, channels)
            grad_pre[t] = cube
            edge_out[t] = jnp.where(tile == 0, cube[height - 1], cube[0])
        turned[p] = jnp.concatenate([outs[0][1], outs[1][1]], axis=1).T
        total[...] += summed
        leave(p).start()

    @pl.loop(0, frames // 2 - 1)
    def _(p):
        leave(p).wait()


STEP = 32
GROUP = 12
HALVES = (
    (
        (*range(0, 12), 24, 25),
        (*range(36, 48), 27, 28),
        (*range(60, 74),),
        (*range(84, 96), 81, 82),
    ),
    (
        (*range(12, 24), 26),
        (*range(29, 36), *range(48, 54)),
        (*range(54, 60), *range(74, 81)),
        (*range(96, 108), 83),
    ),
)
LEAVING = (0x866421, 0x765320)
STAYING = (0x7530, 0x8841)
COUNTS = {LEAVING: (6, 3), STAYING: (4, 4)}


def runs_of(steps):
    runs = []
    for position, step in enumerate(steps):
        if runs and step == runs[-1][1] + runs[-1][2] and step % GROUP:
            runs[-1][2] += 1
        else:
            runs.append([position, step, 1])
    return runs


def place_half(target, half, blocks, total, me):
    for j, steps in enumerate(HALVES[half]):
        spot = me ^ j
        for position, step, count in runs_of(steps):
            g, at = step // GROUP, step % GROUP * STEP
            target[spot, position * STEP : (position + count) * STEP] = blocks(
                g, at, at + count * STEP
            )
        if half == 1:
            line = jnp.concatenate(
                [total, jnp.zeros((STEP - 1, total.shape[1]), F32)], axis=0
            ).astype(BF16)
            target[spot, len(steps) * STEP : (len(steps) + 1) * STEP] = line


def group_loop(codes, front, windows, grads, blocks, tile):
    channels = grads.shape[0]
    frames = windows.shape[0]
    height = windows.shape[1] - 2
    code = jnp.where(tile == 0, codes[0], codes[1])
    count, together = COUNTS[codes]

    @pl.loop(0, count // together)
    def _(i):
        for k in range(together):
            g = lax.shift_right_logical(code, 4 * (together * i + k)) & 15
            a, b = g // 3, g % 3
            source = jnp.concatenate(
                [
                    (
                        front[t + a, pl.ds(b, height)]
                        if t < 2
                        else windows[t - 2 + a, pl.ds(b, height)]
                    ).reshape(-1, 3 * channels)
                    for s in range(2)
                    for t in range(s, frames, 2)
                ],
                axis=0,
            )
            product = jnp.dot(grads[...], source, preferred_element_type=F32).astype(BF16)
            for e in range(3):
                lanes = slice(e * channels, (e + 1) * channels)
                blocks[g, lanes] = product[:, lanes].T


def first_frames(
    x, before, bias, cotangent, windows, taps, turned, edge_in, total, block_out, grad_pre, edge_out,
    early, bias_here, upstream, result, arriving, leaving,
):
    frames, height, breadth, channels = x.shape
    tile = lax.axis_index("tile")
    bias_copy = pltpu.make_async_copy(bias, bias_here, arriving.at[0])
    up_copy = pltpu.make_async_copy(cotangent.at[0:2], upstream, arriving.at[1])
    bias_copy.start()
    up_copy.start()
    for f in range(2):
        fill_windows(early, f, before[f * height : (f + 1) * height], before[2 * height + f], tile)
    bias_copy.wait()
    up_copy.wait()
    summed = total[...]
    firsts = forward_pair(
        [early[0], early[1], windows[0], windows[1]],
        taps,
        bias_here,
        [x[0], x[1]],
        [upstream[0], upstream[1]],
    )
    for s in range(2):
        result[s] = firsts[s][0].reshape(height, breadth, channels)
        cube = firsts[s][1].reshape(height, breadth, channels)
        summed = summed + jnp.sum(firsts[s][1].astype(F32), axis=0, keepdims=True)
        grad_pre[s] = cube
        edge_out[s] = jnp.where(tile == 0, cube[height - 1], cube[0])
    edge_out[2:frames] = edge_in[...]
    copy = pltpu.make_async_copy(result, block_out.at[0:2], leaving)
    copy.start()
    grads = jnp.concatenate(
        [
            part
            for s in range(2)
            for part in [firsts[s][1].T]
            + [turned[p, s * channels : (s + 1) * channels] for p in range(frames // 2 - 1)]
        ],
        axis=1,
    )
    return grads, summed, copy


def leaving_half_kernel(
    block_in, x, before, bias, cotangent, windows, taps, turned, edge_in, total,
    block_out, grad_pre, edge_out, sent, blocks, front, grads, total_out,
    bias_here, upstream, result, arriving, leaving,
):
    tile = lax.axis_index("tile")
    me = lax.axis_index("dp")
    front[2:4] = windows[0:2]
    values, summed, copy = first_frames(
        x, before, bias, cotangent, windows, taps, turned, edge_in, total, block_out, grad_pre, edge_out,
        front, bias_here, upstream, result, arriving, leaving,
    )
    grads[...] = values
    total_out[...] = summed
    group_loop(LEAVING, front, windows, grads, blocks, tile)
    for own in range(2):

        @pl.when(tile == own)
        def _():
            place_half(sent, 1 - own, lambda g, low, high: blocks[g, low:high], summed, me)

    copy.wait()


def staying_half_kernel(blocks_in, front, windows, grads, total, kept, blocks):
    tile = lax.axis_index("tile")
    me = lax.axis_index("dp")
    group_loop(STAYING, front, windows, grads, blocks, tile)
    for own in range(2):
        mine = [STAYING[own] >> 4 * i & 15 for i in range(COUNTS[STAYING][0])]

        @pl.when(tile == own)
        def _():
            place_half(
                kept,
                own,
                lambda g, low, high: (blocks if g in mine else blocks_in)[g, low:high],
                total[...],
                me,
            )


def whole_weights_kernel(
    block_in, x, before, bias, cotangent, windows, taps, turned, edge_in, total,
    block_out, grad_pre, edge_out, weights, bias_sum,
    early, bias_here, upstream, result, arriving, leaving,
):
    frames, height, breadth, channels = x.shape
    grads, summed, copy = first_frames(
        x, before, bias, cotangent, windows, taps, turned, edge_in, total, block_out, grad_pre, edge_out,
        early, bias_here, upstream, result, arriving, leaving,
    )
    for b in range(3):
        for a in range(3):
            source = jnp.concatenate(
                [
                    (early[t + a, b : b + height] if t + a < 2 else windows[t + a - 2, b : b + height])
                    .reshape(-1, 3 * channels)
                    for s in range(2)
                    for t in range(s, frames, 2)
                ],
                axis=0,
            )
            product = jnp.dot(grads, source, preferred_element_type=F32).astype(BF16)
            for e in range(3):
                weights[(a * 3 + b) * 3 + e] = product[:, e * channels : (e + 1) * channels].T
    bias_sum[...] = summed
    copy.wait()


def back_pair(frames, taps, upstream):
    back = lax.dot_general(
        window_block(frames), taps[...], (((1,), (1,)), ((), ())), preferred_element_type=F32
    )
    channels = back.shape[1] // 2
    return [
        (
            upstream[s].astype(F32)
            + back[:, s * channels : (s + 1) * channels].reshape(upstream[s].shape)
        ).astype(BF16)
        for s in range(2)
    ]


def back_interior_kernel(
    early, g, edge, kernel, cotangent, grad_input, last, taps, windows, upstream, result, arriving, leaving
):
    frames, height, breadth, channels = cotangent.shape
    tile = lax.axis_index("tile")
    up_copy = pltpu.make_async_copy(cotangent.at[0 : frames - 2], upstream, arriving)
    up_copy.start()
    for f in range(4):
        for s in range(2):
            a = 2 - f + s
            for b in range(3):
                for e in range(3):
                    lanes = ((f * 3 + b) * 3 + e) * channels
                    where = (slice(s * channels, (s + 1) * channels), slice(lanes, lanes + channels))
                    if 0 <= a < 3:
                        k = ((a * 3 + 2 - b) * 3 + 2 - e) * channels
                        taps[where] = kernel[k : k + channels]
                    else:
                        taps[where] = jnp.zeros((channels, channels), BF16)
    for f in range(2):
        fill_windows(windows, f, early[f], edge[f], tile)

    @pl.loop(2, frames)
    def _(f):
        fill_windows(windows, f, g[f - 2], edge[f], tile)

    last[...] = windows[frames - 2 : frames]
    up_copy.wait()

    def leave(p):
        return pltpu.make_async_copy(
            result.at[pl.ds(2 * p, 2)], grad_input.at[pl.ds(2 * p, 2)], leaving
        )

    @pl.loop(0, frames // 2 - 1)
    def _(p):
        pair = back_pair(
            [windows[2 * p + f] for f in range(4)],
            taps,
            [upstream[2 * p], upstream[2 * p + 1]],
        )
        for s in range(2):
            result[2 * p + s] = pair[s]
        leave(p).start()

    @pl.loop(0, frames // 2 - 1)
    def _(p):
        leave(p).wait()


def back_last_kernel(
    grad_in, last, after, taps, cotangent, grad_input, windows, upstream, result, arriving, leaving
):
    frames, height, breadth, channels = cotangent.shape
    tile = lax.axis_index("tile")
    up_copy = pltpu.make_async_copy(cotangent.at[frames - 2 : frames], upstream, arriving)
    up_copy.start()
    for f in range(2):
        fill_windows(windows, f, after[f * height : (f + 1) * height], after[2 * height + f], tile)
    up_copy.wait()
    pair = back_pair(
        [last[0], last[1], windows[0], windows[1]], taps, [upstream[0], upstream[1]]
    )
    for s in range(2):
        result[s] = pair[s]
    copy = pltpu.make_async_copy(result, grad_input.at[frames - 2 : frames], leaving)
    copy.start()
    copy.wait()


def border_kernel(x, edge, tail, copied):
    frames, height = x.shape[:2]
    row = jnp.where(lax.axis_index("tile") == 0, height - 1, 0)
    copies = [
        pltpu.make_async_copy(x.at[:, row], edge, copied.at[0]),
        pltpu.make_async_copy(x.at[frames - 2 : frames], tail, copied.at[1]),
    ]
    for copy in copies:
        copy.start()
    for copy in copies:
        copy.wait()


def closing_kernel(own, other, weight, bias, *, scale, arranged):
    tile = lax.axis_index("tile")
    me = lax.axis_index("dp")
    half, channels = own.shape
    mine, theirs = own[...].astype(F32) * scale, other[...].astype(F32) * scale
    halves = jnp.where(tile == 0, mine, theirs), jnp.where(tile == 0, theirs, mine)
    if arranged:
        per = weight.shape[0] // STEP
        at = (len(HALVES[1][0]) * STEP) % half
        for j in range(len(HALVES[0])):

            @pl.when(me == j)
            def _():
                for h in range(2):
                    for position, step, count in runs_of(HALVES[h][j]):
                        q = (step - j * per) * STEP
                        weight[q : q + count * STEP] = halves[h][
                            position * STEP : (position + count) * STEP
                        ]

    else:
        at = weight.shape[0] - half
        weight[0:half] = halves[0]
        weight[half:] = halves[1][0:at]
    line = halves[1][at : at + 1]
    share = bias.shape[1]
    picked = jnp.zeros((1, share), F32)
    for j in range(channels // share):
        picked = jnp.where(me == j, line[:, j * share : (j + 1) * share], picked)
    bias[...] = picked


def bits_of(count):
    return count.bit_length() - 1


def place_of(me, shard, count, tile):
    apart = me ^ shard
    n = bits_of(count)
    plain = apart * 0
    turned = apart * 0
    for k in range(n):
        bit = (apart >> k) & 1
        plain = plain | (bit << (n - 1 - k))
        turned = turned | (bit << k)
    return jnp.where(tile == 0, plain, turned)


def exchange(block, axis, count, bits):
    route = []
    for i in range(count):
        for c in range(2):
            route.append((i * 2 + c, (i ^ bits[c]) * 2 + c))
    return lax.ppermute(block, (axis, "tile"), route)


def added(a, b):
    return (a.astype(F32) + b.astype(F32)).astype(BF16)


def passed_along(block, axis, distance):
    count = lax.axis_size(axis)
    route = [(i - distance, i) for i in range(count) if 0 <= i - distance < count]
    return lax.ppermute(block, axis, route)


def swapped(block):
    return lax.ppermute(block, "tile", [(0, 1), (1, 0)])


def body(activations, kernel, conv_bias, cotangent):
    clip_count, frames, height, breadth, channels = activations.shape
    x, upstream = activations[0], cotangent[0]
    tile = lax.axis_index("tile")
    shards = lax.axis_size("dp")
    steps = lax.axis_size("tm")
    share = 27 * channels // shards
    half = -(-(share + 1) // 32) * 16
    arranged = shards == 4 and channels == 128

    area = height * breadth
    bias = conv_bias.reshape(1, channels)
    cells = jax.ShapeDtypeStruct(x.shape, BF16)

    def arrays(*shapes, kind=BF16):
        return [jax.ShapeDtypeStruct(shape, kind) for shape in shapes]

    def windows_shape(count):
        return (count, height + 2, breadth, 3 * channels)

    def frames_shape(count):
        return (count, height, breadth, channels)

    def call(kernel_body, name, share, shapes, scratch, far_in, far_out, args, aliases=None):
        here, there = pl.BlockSpec(memory_space=pltpu.VMEM), pl.BlockSpec(memory_space=pltpu.HBM)
        return pl.pallas_call(
            kernel_body,
            out_shape=shapes,
            in_specs=[there if i in far_in else here for i in range(len(args))],
            out_specs=[there if i in far_out else here for i in range(len(shapes))],
            scratch_shapes=scratch,
            input_output_aliases=aliases or {},
            compiler_params=pltpu.CompilerParams(vmem_limit_bytes=32 * 2**20),
            cost_estimate=pl.CostEstimate(
                flops=int(share * 4 * 27 * channels * channels * frames * area),
                bytes_accessed=4 * 2**20,
                transcendentals=0,
            ),
            name=name,
        )(*args)

    dma, vmem = pltpu.SemaphoreType.DMA, pltpu.VMEM
    edge, tail = call(
        border_kernel,
        "border_rows",
        2.0,
        arrays((frames, breadth, channels), frames_shape(2)),
        [dma((2,))],
        (0,),
        (),
        (x,),
    )
    edge = swapped(edge)
    before = passed_along(
        jnp.concatenate(
            [tail.reshape(2 * height, breadth, channels), edge[frames - 2 :]], axis=0
        ),
        "tm",
        1,
    )
    block_out, windows, taps, turned, later_grads, later_edge, total = call(
        interior_kernel,
        "forward_interior",
        0.75,
        [cells]
        + arrays(
            windows_shape(frames),
            (36 * channels, 2 * channels),
            (frames // 2 - 1, 2 * channels, area),
            frames_shape(frames - 2),
            (frames - 2, breadth, channels),
        )
        + arrays((1, channels), kind=F32),
        [
            vmem((1, channels), F32),
            vmem(frames_shape(frames - 2), BF16),
            vmem(frames_shape(frames - 2), BF16),
            dma((2,)),
            dma,
        ],
        (3, 4),
        (0,),
        (x, edge, kernel, bias, upstream),
    )
    front_scratch = [
        vmem((1, channels), F32),
        vmem(frames_shape(2), BF16),
        vmem(frames_shape(2), BF16),
        dma((2,)),
        dma,
    ]
    firsts = [cells] + arrays(frames_shape(2), (frames, breadth, channels))
    operands = (
        block_out, x, before, bias, upstream, windows, taps, turned, later_edge, total,
    )
    if arranged:
        groups = arrays((9, 3 * channels, channels))
        block_out, early_grads, grad_edge, sent, blocks, front, grads, total = call(
            leaving_half_kernel,
            "first_frames_and_leaving_half",
            0.8,
            firsts
            + arrays((shards, half, channels))
            + groups
            + arrays(windows_shape(4), (channels, frames * area))
            + arrays((1, channels), kind=F32),
            front_scratch,
            (0, 3, 4),
            (0,),
            operands,
            {0: 0},
        )
        (kept,) = call(
            staying_half_kernel,
            "staying_half",
            0.45,
            arrays((shards, half, channels)),
            [vmem((9, 3 * channels, channels), BF16)],
            (),
            (),
            (blocks, front, windows, grads, total),
        )
    else:
        block_out, early_grads, grad_edge, weight, line = call(
            whole_weights_kernel,
            "first_frames_and_weights",
            1.25,
            firsts + arrays((27, channels, channels)) + arrays((1, channels), kind=F32),
            [vmem(windows_shape(2), BF16)] + front_scratch,
            (0, 3, 4),
            (0,),
            operands,
            {0: 0},
        )
        weight = weight.reshape(shards, share, channels)
        line = jnp.broadcast_to(line.astype(BF16)[None], (shards, 1, channels))
        pad = jnp.zeros((shards, 2 * half - share - 1, channels), BF16)
        whole = jnp.concatenate([weight, line, pad], axis=1)
        me = lax.axis_index("dp")
        whole = whole.reshape(shards, 2, half, channels)
        kept, sent = (
            jnp.zeros((shards, half, channels), BF16)
            .at[place_of(me, jnp.arange(shards), shards, side)]
            .set(lax.dynamic_index_in_dim(whole, side, 1, False))
            for side in (tile, 1 - tile)
        )

    total = added(kept, swapped(sent))
    edge = swapped(grad_edge)
    edge, total = lax.optimization_barrier((edge, total))
    grad_input, last, taps = call(
        back_interior_kernel,
        "input_gradient_interior",
        0.75,
        [cells] + arrays(windows_shape(2), (2 * channels, 36 * channels)),
        [
            vmem(windows_shape(frames), BF16),
            vmem(frames_shape(frames - 2), BF16),
            vmem(frames_shape(frames - 2), BF16),
            dma,
            dma,
        ],
        (4,),
        (0,),
        (early_grads, later_grads, edge, kernel, upstream),
    )
    first_edge, last = lax.optimization_barrier((edge[:2], last))
    after = passed_along(
        jnp.concatenate(
            [early_grads.reshape(2 * height, breadth, channels), first_edge], axis=0
        ),
        "tm",
        -1,
    )
    if arranged:
        parts = [exchange(total[k], "dp", shards, (k, k)) for k in (2, 3, 1)]
        total = total[0].astype(F32)
        for part in parts:
            total = total + part.astype(F32)
        total = total.astype(BF16)
    else:
        n = bits_of(shards)
        for k in range(n):
            middle = total.shape[0] // 2
            total = added(
                total[:middle], exchange(total[middle:], "dp", shards, (1 << k, 1 << (n - 1 - k)))
            )
        total = total[0]
    total, grad_input = lax.optimization_barrier((total, grad_input))
    (grad_input,) = call(
        back_last_kernel,
        "input_gradient_last",
        0.25,
        [cells],
        [
            vmem(windows_shape(2), BF16),
            vmem(frames_shape(2), BF16),
            vmem(frames_shape(2), BF16),
            dma,
            dma,
        ],
        (0, 4),
        (0,),
        (grad_input, last, after, taps, upstream),
        {0: 0},
    )
    got = {k: exchange(total, "tm", steps, (k, k if k == 3 else 3 - k)) for k in (3, 2, 1)}
    total = (
        (total.astype(F32) + got[1].astype(F32)) + (got[2].astype(F32) + got[3].astype(F32))
    ).astype(BF16)
    total, grad_input = lax.optimization_barrier((total, grad_input))
    other = swapped(total)
    positions = (
        clip_count * frames * height * breadth * shards * steps * lax.axis_size("tile")
    )
    weight, bias_grad = call(
        functools.partial(closing_kernel, scale=1.0 / math.sqrt(positions), arranged=arranged),
        "scaled_weights",
        0.01,
        arrays((share, channels), (1, channels // shards), kind=F32),
        [],
        (),
        (),
        (total, other),
    )
    return block_out[None], grad_input[None], weight, bias_grad.reshape(channels // shards)


def solution(mesh):
    return jax.shard_map(
        body,
        mesh=mesh,
        in_specs=(P("dp", "tm", "tile", None, None), P(), P(), P("dp", "tm", "tile", None, None)),
        out_specs=(
            P("dp", "tm", "tile", None, None),
            P("dp", "tm", "tile", None, None),
            P("dp", None),
            P("dp"),
        ),
        check_vma=False,
    )
```

```python
import functools
import math

import jax
import jax.numpy as jnp
from jax import lax
from jax.experimental import pallas as pl
from jax.experimental.pallas import tpu as pltpu
from jax.sharding import PartitionSpec as P

F32 = jnp.float32
BF16 = jnp.bfloat16


def shifted_columns(cells, breadth):
    count = cells.shape[0]
    wide = cells.astype(F32)
    column = lax.broadcasted_iota(jnp.int32, cells.shape, 0) % breadth
    left = jnp.where(column == 0, 0.0, pltpu.roll(wide, 1, 0))
    right = jnp.where(column == breadth - 1, 0.0, pltpu.roll(wide, count - 1, 0))
    return left.astype(BF16), cells, right.astype(BF16)


def fill_windows(windows, frame, inner, edge, tile):
    height, breadth, channels = inner.shape
    parts = shifted_columns(inner.reshape(height * breadth, channels), breadth)
    edges = shifted_columns(edge, breadth)
    for e in range(3):
        lanes = slice(e * channels, (e + 1) * channels)
        windows[frame, 1 : height + 1, :, lanes] = parts[e].reshape(height, breadth, channels)
        rim = edges[e]
        none = jnp.zeros_like(rim)
        windows[frame, 0, :, lanes] = jnp.where(tile == 0, none, rim)
        windows[frame, height + 1, :, lanes] = jnp.where(tile == 0, rim, none)


def window_block(frames):
    blocks = []
    for frame in frames:
        height = frame.shape[0] - 2
        for b in range(3):
            blocks.append(frame[b : b + height].reshape(-1, frame.shape[-1]))
    return jnp.concatenate(blocks, axis=1)


def activate(pre, source, upstream):
    sigma = jax.nn.sigmoid(pre)
    result = (source.astype(F32) + pre * sigma).astype(BF16)
    grad = (upstream.astype(F32) * sigma * (1.0 + pre * (1.0 - sigma))).astype(BF16)
    return result, grad


def forward_pair(frames, taps, bias, x_pair, upstream, begun=0.0):
    channels = bias.shape[1]
    both = jnp.concatenate([bias[...], bias[...]], axis=1)
    count = 9 * channels * len(frames)
    pre = both + begun + jnp.dot(window_block(frames), taps[0:count], preferred_element_type=F32)
    return [
        activate(
            pre[:, s * channels : (s + 1) * channels],
            x_pair[s].reshape(-1, channels),
            upstream[s].reshape(-1, channels),
        )
        for s in range(2)
    ]


def interior_kernel(
    x,
    edge,
    kernel,
    bias,
    cotangent,
    block_out,
    windows,
    taps,
    turned,
    grad_pre,
    edge_out,
    total,
    begun,
    bias_here,
    upstream,
    result,
    arriving,
    leaving,
):
    frames, height, breadth, channels = x.shape
    area = height * breadth
    tile = lax.axis_index("tile")
    bias_copy = pltpu.make_async_copy(bias, bias_here, arriving.at[0])
    up_copy = pltpu.make_async_copy(cotangent.at[2:frames], upstream, arriving.at[1])
    bias_copy.start()
    up_copy.start()
    rows = 9 * channels
    taps[0 : 3 * rows, 0:channels] = kernel[...]
    taps[3 * rows :, 0:channels] = jnp.zeros((rows, channels), BF16)
    taps[0:rows, channels:] = jnp.zeros((rows, channels), BF16)
    taps[rows:, channels:] = kernel[...]
    @pl.loop(0, frames)
    def _(f):
        fill_windows(windows, f, x[f], edge[f], tile)

    bias_copy.wait()
    up_copy.wait()
    total[...] = jnp.zeros((1, channels), F32)

    def leave(p):
        return pltpu.make_async_copy(
            result.at[pl.ds(2 * p, 2)], block_out.at[pl.ds(2 * p + 2, 2)], leaving
        )

    @pl.loop(0, frames // 2 - 1, unroll=True)
    def _(p):
        outs = forward_pair(
            [windows[2 * p + f] for f in range(4)],
            taps,
            bias_here,
            [x[2 * p + 2], x[2 * p + 3]],
            [upstream[2 * p], upstream[2 * p + 1]],
        )
        summed = jnp.zeros((1, channels), F32)
        for s in range(2):
            t = 2 * p + s
            result[t] = outs[s][0].reshape(height, breadth, channels)
            grad = outs[s][1]
            summed = summed + jnp.sum(grad.astype(F32), axis=0, keepdims=True)
            cube = grad.reshape(height, breadth, channels)
            grad_pre[t] = cube
            edge_out[t] = jnp.where(tile == 0, cube[height - 1], cube[0])
        turned[p] = jnp.concatenate([outs[0][1], outs[1][1]], axis=1).T
        total[...] += summed
        leave(p).start()

    begun[...] = jnp.dot(
        window_block([windows[0], windows[1]]), taps[2 * rows :], preferred_element_type=F32
    )

    @pl.loop(0, frames // 2 - 1)
    def _(p):
        leave(p).wait()


STEP = 32
GROUP = 12
HALVES = (
    (
        (*range(0, 12), 24, 25),
        (*range(36, 48), 27, 28),
        (*range(60, 74),),
        (*range(84, 96), 81, 82),
    ),
    (
        (*range(12, 24), 26),
        (*range(29, 36), *range(48, 54)),
        (*range(54, 60), *range(74, 81)),
        (*range(96, 108), 83),
    ),
)
LEAVING = (0x864210, 0x765320)
STAYING = (0x753, 0x841)
COUNTS = {LEAVING: (6, 3), STAYING: (3, 3)}


def runs_of(steps):
    runs = []
    for position, step in enumerate(steps):
        if runs and step == runs[-1][1] + runs[-1][2] and step % GROUP:
            runs[-1][2] += 1
        else:
            runs.append([position, step, 1])
    return runs


def place_half(target, half, blocks, total, me):
    for j, steps in enumerate(HALVES[half]):
        spot = me ^ j
        for position, step, count in runs_of(steps):
            g, at = step // GROUP, step % GROUP * STEP
            target[spot, position * STEP : (position + count) * STEP] = blocks(
                g, at, at + count * STEP
            )
        if half == 1:
            line = jnp.concatenate(
                [total, jnp.zeros((STEP - 1, total.shape[1]), F32)], axis=0
            ).astype(BF16)
            target[spot, len(steps) * STEP : (len(steps) + 1) * STEP] = line


def group_loop(codes, front, windows, grads, blocks, tile):
    channels = grads.shape[0]
    frames = windows.shape[0]
    height = windows.shape[1] - 2
    code = jnp.where(tile == 0, codes[0], codes[1])
    count, together = COUNTS[codes]

    @pl.loop(0, count // together)
    def _(i):
        for k in range(together):
            g = lax.shift_right_logical(code, 4 * (together * i + k)) & 15
            a, b = g // 3, g % 3
            source = jnp.concatenate(
                [
                    (
                        front[t + a, pl.ds(b, height)]
                        if t < 2
                        else windows[t - 2 + a, pl.ds(b, height)]
                    ).reshape(-1, 3 * channels)
                    for s in range(2)
                    for t in range(s, frames, 2)
                ],
                axis=0,
            )
            product = jnp.dot(grads[...], source, preferred_element_type=F32).astype(BF16)
            for e in range(3):
                lanes = slice(e * channels, (e + 1) * channels)
                blocks[g, lanes] = product[:, lanes].T


def first_frames(
    x, before, bias, cotangent, windows, taps, turned, edge_in, total, begun, block_out, grad_pre, edge_out,
    early, bias_here, upstream, result, arriving, leaving,
):
    frames, height, breadth, channels = x.shape
    tile = lax.axis_index("tile")
    bias_copy = pltpu.make_async_copy(bias, bias_here, arriving.at[0])
    up_copy = pltpu.make_async_copy(cotangent.at[0:2], upstream, arriving.at[1])
    bias_copy.start()
    up_copy.start()
    for f in range(2):
        fill_windows(early, f, before[f * height : (f + 1) * height], before[2 * height + f], tile)
    bias_copy.wait()
    up_copy.wait()
    summed = total[...]
    firsts = forward_pair(
        [early[0], early[1]],
        taps,
        bias_here,
        [x[0], x[1]],
        [upstream[0], upstream[1]],
        begun[...],
    )
    for s in range(2):
        result[s] = firsts[s][0].reshape(height, breadth, channels)
        cube = firsts[s][1].reshape(height, breadth, channels)
        summed = summed + jnp.sum(firsts[s][1].astype(F32), axis=0, keepdims=True)
        grad_pre[s] = cube
        edge_out[s] = jnp.where(tile == 0, cube[height - 1], cube[0])
    edge_out[2:frames] = edge_in[...]
    copy = pltpu.make_async_copy(result, block_out.at[0:2], leaving)
    copy.start()
    grads = jnp.concatenate(
        [
            part
            for s in range(2)
            for part in [firsts[s][1].T]
            + [turned[p, s * channels : (s + 1) * channels] for p in range(frames // 2 - 1)]
        ],
        axis=1,
    )
    return grads, summed, copy


def leaving_half_kernel(
    block_in, x, before, bias, cotangent, windows, taps, turned, edge_in, total, begun,
    block_out, grad_pre, edge_out, sent, blocks, front, grads, total_out,
    bias_here, upstream, result, arriving, leaving,
):
    tile = lax.axis_index("tile")
    me = lax.axis_index("dp")
    front[2:4] = windows[0:2]
    values, summed, copy = first_frames(
        x, before, bias, cotangent, windows, taps, turned, edge_in, total, begun, block_out, grad_pre, edge_out,
        front, bias_here, upstream, result, arriving, leaving,
    )
    grads[...] = values
    total_out[...] = summed
    group_loop(LEAVING, front, windows, grads, blocks, tile)
    for own in range(2):

        @pl.when(tile == own)
        def _():
            place_half(sent, 1 - own, lambda g, low, high: blocks[g, low:high], summed, me)

    copy.wait()


def staying_half_kernel(blocks_in, front, windows, grads, total, kept, blocks):
    tile = lax.axis_index("tile")
    me = lax.axis_index("dp")
    group_loop(STAYING, front, windows, grads, blocks, tile)
    for own in range(2):
        mine = [STAYING[own] >> 4 * i & 15 for i in range(COUNTS[STAYING][0])]

        @pl.when(tile == own)
        def _():
            place_half(
                kept,
                own,
                lambda g, low, high: (blocks if g in mine else blocks_in)[g, low:high],
                total[...],
                me,
            )


def whole_weights_kernel(
    block_in, x, before, bias, cotangent, windows, taps, turned, edge_in, total, begun,
    block_out, grad_pre, edge_out, weights, bias_sum,
    early, bias_here, upstream, result, arriving, leaving,
):
    frames, height, breadth, channels = x.shape
    grads, summed, copy = first_frames(
        x, before, bias, cotangent, windows, taps, turned, edge_in, total, begun, block_out, grad_pre, edge_out,
        early, bias_here, upstream, result, arriving, leaving,
    )
    for b in range(3):
        for a in range(3):
            source = jnp.concatenate(
                [
                    (early[t + a, b : b + height] if t + a < 2 else windows[t + a - 2, b : b + height])
                    .reshape(-1, 3 * channels)
                    for s in range(2)
                    for t in range(s, frames, 2)
                ],
                axis=0,
            )
            product = jnp.dot(grads, source, preferred_element_type=F32).astype(BF16)
            for e in range(3):
                weights[(a * 3 + b) * 3 + e] = product[:, e * channels : (e + 1) * channels].T
    bias_sum[...] = summed
    copy.wait()


def back_pair(frames, taps, upstream):
    back = lax.dot_general(
        window_block(frames), taps[...], (((1,), (1,)), ((), ())), preferred_element_type=F32
    )
    channels = back.shape[1] // 2
    return [
        (
            upstream[s].astype(F32)
            + back[:, s * channels : (s + 1) * channels].reshape(upstream[s].shape)
        ).astype(BF16)
        for s in range(2)
    ]


def back_interior_kernel(
    early, g, edge, kernel, cotangent, grad_input, last, taps, windows, upstream, result, arriving, leaving
):
    frames, height, breadth, channels = cotangent.shape
    tile = lax.axis_index("tile")
    up_copy = pltpu.make_async_copy(cotangent.at[0 : frames - 2], upstream, arriving)
    up_copy.start()
    for f in range(4):
        for s in range(2):
            a = 2 - f + s
            for b in range(3):
                for e in range(3):
                    lanes = ((f * 3 + b) * 3 + e) * channels
                    where = (slice(s * channels, (s + 1) * channels), slice(lanes, lanes + channels))
                    if 0 <= a < 3:
                        k = ((a * 3 + 2 - b) * 3 + 2 - e) * channels
                        taps[where] = kernel[k : k + channels]
                    else:
                        taps[where] = jnp.zeros((channels, channels), BF16)
    for f in range(2):
        fill_windows(windows, f, early[f], edge[f], tile)

    @pl.loop(2, frames)
    def _(f):
        fill_windows(windows, f, g[f - 2], edge[f], tile)

    last[...] = windows[frames - 2 : frames]
    up_copy.wait()

    def leave(p):
        return pltpu.make_async_copy(
            result.at[pl.ds(2 * p, 2)], grad_input.at[pl.ds(2 * p, 2)], leaving
        )

    @pl.loop(0, frames // 2 - 1)
    def _(p):
        pair = back_pair(
            [windows[2 * p + f] for f in range(4)],
            taps,
            [upstream[2 * p], upstream[2 * p + 1]],
        )
        for s in range(2):
            result[2 * p + s] = pair[s]
        leave(p).start()

    @pl.loop(0, frames // 2 - 1)
    def _(p):
        leave(p).wait()


def back_last_kernel(
    grad_in, last, after, taps, cotangent, grad_input, windows, upstream, result, arriving, leaving
):
    frames, height, breadth, channels = cotangent.shape
    tile = lax.axis_index("tile")
    up_copy = pltpu.make_async_copy(cotangent.at[frames - 2 : frames], upstream, arriving)
    up_copy.start()
    for f in range(2):
        fill_windows(windows, f, after[f * height : (f + 1) * height], after[2 * height + f], tile)
    up_copy.wait()
    pair = back_pair(
        [last[0], last[1], windows[0], windows[1]], taps, [upstream[0], upstream[1]]
    )
    for s in range(2):
        result[s] = pair[s]
    copy = pltpu.make_async_copy(result, grad_input.at[frames - 2 : frames], leaving)
    copy.start()
    copy.wait()


def border_kernel(x, edge, tail, copied):
    frames, height = x.shape[:2]
    row = jnp.where(lax.axis_index("tile") == 0, height - 1, 0)
    copies = [
        pltpu.make_async_copy(x.at[:, row], edge, copied.at[0]),
        pltpu.make_async_copy(x.at[frames - 2 : frames], tail, copied.at[1]),
    ]
    for copy in copies:
        copy.start()
    for copy in copies:
        copy.wait()


def closing_kernel(own, other, weight, bias, *, scale, arranged):
    tile = lax.axis_index("tile")
    me = lax.axis_index("dp")
    half, channels = own.shape
    mine, theirs = own[...].astype(F32) * scale, other[...].astype(F32) * scale
    halves = jnp.where(tile == 0, mine, theirs), jnp.where(tile == 0, theirs, mine)
    if arranged:
        per = weight.shape[0] // STEP
        at = (len(HALVES[1][0]) * STEP) % half
        for j in range(len(HALVES[0])):

            @pl.when(me == j)
            def _():
                for h in range(2):
                    for position, step, count in runs_of(HALVES[h][j]):
                        q = (step - j * per) * STEP
                        weight[q : q + count * STEP] = halves[h][
                            position * STEP : (position + count) * STEP
                        ]

    else:
        at = weight.shape[0] - half
        weight[0:half] = halves[0]
        weight[half:] = halves[1][0:at]
    line = halves[1][at : at + 1]
    share = bias.shape[1]
    picked = jnp.zeros((1, share), F32)
    for j in range(channels // share):
        picked = jnp.where(me == j, line[:, j * share : (j + 1) * share], picked)
    bias[...] = picked


def bits_of(count):
    return count.bit_length() - 1


def place_of(me, shard, count, tile):
    apart = me ^ shard
    n = bits_of(count)
    plain = apart * 0
    turned = apart * 0
    for k in range(n):
        bit = (apart >> k) & 1
        plain = plain | (bit << (n - 1 - k))
        turned = turned | (bit << k)
    return jnp.where(tile == 0, plain, turned)


def exchange(block, axis, count, bits):
    route = []
    for i in range(count):
        for c in range(2):
            route.append((i * 2 + c, (i ^ bits[c]) * 2 + c))
    return lax.ppermute(block, (axis, "tile"), route)


def added(a, b):
    return (a.astype(F32) + b.astype(F32)).astype(BF16)


def passed_along(block, axis, distance):
    count = lax.axis_size(axis)
    route = [(i - distance, i) for i in range(count) if 0 <= i - distance < count]
    return lax.ppermute(block, axis, route)


def swapped(block):
    return lax.ppermute(block, "tile", [(0, 1), (1, 0)])


def body(activations, kernel, conv_bias, cotangent):
    clip_count, frames, height, breadth, channels = activations.shape
    x, upstream = activations[0], cotangent[0]
    tile = lax.axis_index("tile")
    shards = lax.axis_size("dp")
    steps = lax.axis_size("tm")
    share = 27 * channels // shards
    half = -(-(share + 1) // 32) * 16
    arranged = shards == 4 and channels == 128

    area = height * breadth
    bias = conv_bias.reshape(1, channels)
    cells = jax.ShapeDtypeStruct(x.shape, BF16)

    def arrays(*shapes, kind=BF16):
        return [jax.ShapeDtypeStruct(shape, kind) for shape in shapes]

    def windows_shape(count):
        return (count, height + 2, breadth, 3 * channels)

    def frames_shape(count):
        return (count, height, breadth, channels)

    def call(kernel_body, name, share, shapes, scratch, far_in, far_out, args, aliases=None):
        here, there = pl.BlockSpec(memory_space=pltpu.VMEM), pl.BlockSpec(memory_space=pltpu.HBM)
        return pl.pallas_call(
            kernel_body,
            out_shape=shapes,
            in_specs=[there if i in far_in else here for i in range(len(args))],
            out_specs=[there if i in far_out else here for i in range(len(shapes))],
            scratch_shapes=scratch,
            input_output_aliases=aliases or {},
            compiler_params=pltpu.CompilerParams(vmem_limit_bytes=32 * 2**20),
            cost_estimate=pl.CostEstimate(
                flops=int(share * 4 * 27 * channels * channels * frames * area),
                bytes_accessed=4 * 2**20,
                transcendentals=0,
            ),
            name=name,
        )(*args)

    dma, vmem = pltpu.SemaphoreType.DMA, pltpu.VMEM
    edge, tail = call(
        border_kernel,
        "border_rows",
        2.0,
        arrays((frames, breadth, channels), frames_shape(2)),
        [dma((2,))],
        (0,),
        (),
        (x,),
    )
    edge = swapped(edge)
    before = passed_along(
        jnp.concatenate(
            [tail.reshape(2 * height, breadth, channels), edge[frames - 2 :]], axis=0
        ),
        "tm",
        1,
    )
    block_out, windows, taps, turned, later_grads, later_edge, total, begun = call(
        interior_kernel,
        "forward_interior",
        0.75,
        [cells]
        + arrays(
            windows_shape(frames),
            (36 * channels, 2 * channels),
            (frames // 2 - 1, 2 * channels, area),
            frames_shape(frames - 2),
            (frames - 2, breadth, channels),
        )
        + arrays((1, channels), (area, 2 * channels), kind=F32),
        [
            vmem((1, channels), F32),
            vmem(frames_shape(frames - 2), BF16),
            vmem(frames_shape(frames - 2), BF16),
            dma((2,)),
            dma,
        ],
        (3, 4),
        (0,),
        (x, edge, kernel, bias, upstream),
    )
    front_scratch = [
        vmem((1, channels), F32),
        vmem(frames_shape(2), BF16),
        vmem(frames_shape(2), BF16),
        dma((2,)),
        dma,
    ]
    firsts = [cells] + arrays(frames_shape(2), (frames, breadth, channels))
    operands = (
        block_out, x, before, bias, upstream, windows, taps, turned, later_edge, total, begun,
    )
    if arranged:
        groups = arrays((9, 3 * channels, channels))
        block_out, early_grads, grad_edge, sent, blocks, front, grads, total = call(
            leaving_half_kernel,
            "first_frames_and_leaving_half",
            0.8,
            firsts
            + arrays((shards, half, channels))
            + groups
            + arrays(windows_shape(4), (channels, frames * area))
            + arrays((1, channels), kind=F32),
            front_scratch,
            (0, 3, 4),
            (0,),
            operands,
            {0: 0},
        )
        (kept,) = call(
            staying_half_kernel,
            "staying_half",
            0.45,
            arrays((shards, half, channels)),
            [vmem((9, 3 * channels, channels), BF16)],
            (),
            (),
            (blocks, front, windows, grads, total),
        )
    else:
        block_out, early_grads, grad_edge, weight, line = call(
            whole_weights_kernel,
            "first_frames_and_weights",
            1.25,
            firsts + arrays((27, channels, channels)) + arrays((1, channels), kind=F32),
            [vmem(windows_shape(2), BF16)] + front_scratch,
            (0, 3, 4),
            (0,),
            operands,
            {0: 0},
        )
        weight = weight.reshape(shards, share, channels)
        line = jnp.broadcast_to(line.astype(BF16)[None], (shards, 1, channels))
        pad = jnp.zeros((shards, 2 * half - share - 1, channels), BF16)
        whole = jnp.concatenate([weight, line, pad], axis=1)
        me = lax.axis_index("dp")
        whole = whole.reshape(shards, 2, half, channels)
        kept, sent = (
            jnp.zeros((shards, half, channels), BF16)
            .at[place_of(me, jnp.arange(shards), shards, side)]
            .set(lax.dynamic_index_in_dim(whole, side, 1, False))
            for side in (tile, 1 - tile)
        )

    total = added(kept, swapped(sent))
    edge = swapped(grad_edge)
    edge, total = lax.optimization_barrier((edge, total))
    grad_input, last, taps = call(
        back_interior_kernel,
        "input_gradient_interior",
        0.75,
        [cells] + arrays(windows_shape(2), (2 * channels, 36 * channels)),
        [
            vmem(windows_shape(frames), BF16),
            vmem(frames_shape(frames - 2), BF16),
            vmem(frames_shape(frames - 2), BF16),
            dma,
            dma,
        ],
        (4,),
        (0,),
        (early_grads, later_grads, edge, kernel, upstream),
    )
    first_edge, last = lax.optimization_barrier((edge[:2], last))
    after = passed_along(
        jnp.concatenate(
            [early_grads.reshape(2 * height, breadth, channels), first_edge], axis=0
        ),
        "tm",
        -1,
    )
    if arranged:
        parts = [exchange(total[k], "dp", shards, (k, k)) for k in (2, 3, 1)]
        total = total[0].astype(F32)
        for part in parts:
            total = total + part.astype(F32)
        total = total.astype(BF16)
    else:
        n = bits_of(shards)
        for k in range(n):
            middle = total.shape[0] // 2
            total = added(
                total[:middle], exchange(total[middle:], "dp", shards, (1 << k, 1 << (n - 1 - k)))
            )
        total = total[0]
    total, grad_input = lax.optimization_barrier((total, grad_input))
    (grad_input,) = call(
        back_last_kernel,
        "input_gradient_last",
        0.25,
        [cells],
        [
            vmem(windows_shape(2), BF16),
            vmem(frames_shape(2), BF16),
            vmem(frames_shape(2), BF16),
            dma,
            dma,
        ],
        (0, 4),
        (0,),
        (grad_input, last, after, taps, upstream),
        {0: 0},
    )
    got = {k: exchange(total, "tm", steps, (k, k if k == 3 else 3 - k)) for k in (3, 2, 1)}
    total = (
        (total.astype(F32) + got[1].astype(F32)) + (got[2].astype(F32) + got[3].astype(F32))
    ).astype(BF16)
    total, grad_input = lax.optimization_barrier((total, grad_input))
    other = swapped(total)
    positions = (
        clip_count * frames * height * breadth * shards * steps * lax.axis_size("tile")
    )
    weight, bias_grad = call(
        functools.partial(closing_kernel, scale=1.0 / math.sqrt(positions), arranged=arranged),
        "scaled_weights",
        0.01,
        arrays((share, channels), (1, channels // shards), kind=F32),
        [],
        (),
        (),
        (total, other),
    )
    return block_out[None], grad_input[None], weight, bias_grad.reshape(channels // shards)


def solution(mesh):
    return jax.shard_map(
        body,
        mesh=mesh,
        in_specs=(P("dp", "tm", "tile", None, None), P(), P(), P("dp", "tm", "tile", None, None)),
        out_specs=(
            P("dp", "tm", "tile", None, None),
            P("dp", "tm", "tile", None, None),
            P("dp", None),
            P("dp"),
        ),
        check_vma=False,
    )
```

```python
import functools
import math

import jax
import jax.numpy as jnp
from jax import lax
from jax.experimental import pallas as pl
from jax.experimental.pallas import tpu as pltpu
from jax.sharding import PartitionSpec as P

F32 = jnp.float32
BF16 = jnp.bfloat16


def shifted_columns(cells, breadth):
    count = cells.shape[0]
    wide = cells.astype(F32)
    column = lax.broadcasted_iota(jnp.int32, cells.shape, 0) % breadth
    left = jnp.where(column == 0, 0.0, pltpu.roll(wide, 1, 0))
    right = jnp.where(column == breadth - 1, 0.0, pltpu.roll(wide, count - 1, 0))
    return left.astype(BF16), cells, right.astype(BF16)


def fill_windows(windows, frame, inner, edge, tile):
    height, breadth, channels = inner.shape
    parts = shifted_columns(inner.reshape(height * breadth, channels), breadth)
    edges = shifted_columns(edge, breadth)
    for e in range(3):
        lanes = slice(e * channels, (e + 1) * channels)
        windows[frame, 1 : height + 1, :, lanes] = parts[e].reshape(height, breadth, channels)
        rim = edges[e]
        none = jnp.zeros_like(rim)
        windows[frame, 0, :, lanes] = jnp.where(tile == 0, none, rim)
        windows[frame, height + 1, :, lanes] = jnp.where(tile == 0, rim, none)


def window_block(frames):
    blocks = []
    for frame in frames:
        height = frame.shape[0] - 2
        for b in range(3):
            blocks.append(frame[b : b + height].reshape(-1, frame.shape[-1]))
    return jnp.concatenate(blocks, axis=1)


def activate(pre, source, upstream):
    sigma = jax.nn.sigmoid(pre)
    result = (source.astype(F32) + pre * sigma).astype(BF16)
    grad = (upstream.astype(F32) * sigma * (1.0 + pre * (1.0 - sigma))).astype(BF16)
    return result, grad


def forward_pair(frames, taps, bias, x_pair, upstream, begun=0.0):
    channels = bias.shape[1]
    both = jnp.concatenate([bias[...], bias[...]], axis=1)
    count = 9 * channels * len(frames)
    pre = both + begun + jnp.dot(window_block(frames), taps[0:count], preferred_element_type=F32)
    return [
        activate(
            pre[:, s * channels : (s + 1) * channels],
            x_pair[s].reshape(-1, channels),
            upstream[s].reshape(-1, channels),
        )
        for s in range(2)
    ]


def interior_kernel(
    x,
    edge,
    kernel,
    bias,
    cotangent,
    block_out,
    windows,
    taps,
    turned,
    grad_pre,
    edge_out,
    total,
    begun,
    bias_here,
    upstream,
    result,
    arriving,
    leaving,
):
    frames, height, breadth, channels = x.shape
    area = height * breadth
    tile = lax.axis_index("tile")
    bias_copy = pltpu.make_async_copy(bias, bias_here, arriving.at[0])
    up_copy = pltpu.make_async_copy(cotangent.at[2:frames], upstream, arriving.at[1])
    bias_copy.start()
    up_copy.start()
    rows = 9 * channels
    taps[0 : 3 * rows, 0:channels] = kernel[...]
    taps[3 * rows :, 0:channels] = jnp.zeros((rows, channels), BF16)
    taps[0:rows, channels:] = jnp.zeros((rows, channels), BF16)
    taps[rows:, channels:] = kernel[...]
    @pl.loop(0, frames)
    def _(f):
        fill_windows(windows, f, x[f], edge[f], tile)

    bias_copy.wait()
    up_copy.wait()
    total[...] = jnp.zeros((1, channels), F32)

    def leave(p):
        return pltpu.make_async_copy(
            result.at[pl.ds(2 * p, 2)], block_out.at[pl.ds(2 * p + 2, 2)], leaving
        )

    @pl.loop(0, frames // 2 - 1, unroll=True)
    def _(p):
        outs = forward_pair(
            [windows[2 * p + f] for f in range(4)],
            taps,
            bias_here,
            [x[2 * p + 2], x[2 * p + 3]],
            [upstream[2 * p], upstream[2 * p + 1]],
        )
        summed = jnp.zeros((1, channels), F32)
        for s in range(2):
            t = 2 * p + s
            result[t] = outs[s][0].reshape(height, breadth, channels)
            grad = outs[s][1]
            summed = summed + jnp.sum(grad.astype(F32), axis=0, keepdims=True)
            cube = grad.reshape(height, breadth, channels)
            grad_pre[t] = cube
            edge_out[t] = jnp.where(tile == 0, cube[height - 1], cube[0])
        turned[p] = jnp.concatenate([outs[0][1], outs[1][1]], axis=1).T
        total[...] += summed
        leave(p).start()

    begun[...] = jnp.dot(
        window_block([windows[0], windows[1]]), taps[2 * rows :], preferred_element_type=F32
    )

    @pl.loop(0, frames // 2 - 1)
    def _(p):
        leave(p).wait()


STEP = 32
GROUP = 12
HALVES = (
    (
        (*range(0, 12), 24, 25),
        (*range(36, 48), 27, 28),
        (*range(60, 74),),
        (*range(84, 96), 81, 82),
    ),
    (
        (*range(12, 24), 26),
        (*range(29, 36), *range(48, 54)),
        (*range(54, 60), *range(74, 81)),
        (*range(96, 108), 83),
    ),
)
LEAVING = (0x864210, 0x765320)
STAYING = (0x753, 0x841)
COUNTS = {LEAVING: (6, 3), STAYING: (3, 3)}


def runs_of(steps):
    runs = []
    for position, step in enumerate(steps):
        if runs and step == runs[-1][1] + runs[-1][2] and step % GROUP:
            runs[-1][2] += 1
        else:
            runs.append([position, step, 1])
    return runs


def place_half(target, half, blocks, total, me):
    for j, steps in enumerate(HALVES[half]):
        spot = me ^ j
        for position, step, count in runs_of(steps):
            g, at = step // GROUP, step % GROUP * STEP
            target[spot, position * STEP : (position + count) * STEP] = blocks(
                g, at, at + count * STEP
            )
        if half == 1:
            line = jnp.concatenate(
                [total, jnp.zeros((STEP - 1, total.shape[1]), F32)], axis=0
            ).astype(BF16)
            target[spot, len(steps) * STEP : (len(steps) + 1) * STEP] = line


def group_loop(codes, front, windows, grads, blocks, tile):
    channels = grads.shape[0]
    frames = windows.shape[0]
    height = windows.shape[1] - 2
    code = jnp.where(tile == 0, codes[0], codes[1])
    count, together = COUNTS[codes]

    @pl.loop(0, count // together)
    def _(i):
        for k in range(together):
            g = lax.shift_right_logical(code, 4 * (together * i + k)) & 15
            a, b = g // 3, g % 3
            source = jnp.concatenate(
                [
                    (
                        front[t + a, pl.ds(b, height)]
                        if t < 2
                        else windows[t - 2 + a, pl.ds(b, height)]
                    ).reshape(-1, 3 * channels)
                    for s in range(2)
                    for t in range(s, frames, 2)
                ],
                axis=0,
            )
            product = jnp.dot(grads[...], source, preferred_element_type=F32).astype(BF16)
            for e in range(3):
                lanes = slice(e * channels, (e + 1) * channels)
                blocks[g, lanes] = product[:, lanes].T


def first_frames(
    x, before, bias, cotangent, windows, taps, turned, edge_in, total, begun, block_out, grad_pre, edge_out,
    early, bias_here, upstream, result, arriving, leaving,
):
    frames, height, breadth, channels = x.shape
    tile = lax.axis_index("tile")
    bias_copy = pltpu.make_async_copy(bias, bias_here, arriving.at[0])
    up_copy = pltpu.make_async_copy(cotangent.at[0:2], upstream, arriving.at[1])
    bias_copy.start()
    up_copy.start()
    for f in range(2):
        fill_windows(early, f, before[f * height : (f + 1) * height], before[2 * height + f], tile)
    bias_copy.wait()
    up_copy.wait()
    summed = total[...]
    firsts = forward_pair(
        [early[0], early[1]],
        taps,
        bias_here,
        [x[0], x[1]],
        [upstream[0], upstream[1]],
        begun[...],
    )
    for s in range(2):
        result[s] = firsts[s][0].reshape(height, breadth, channels)
        cube = firsts[s][1].reshape(height, breadth, channels)
        summed = summed + jnp.sum(firsts[s][1].astype(F32), axis=0, keepdims=True)
        grad_pre[s] = cube
        edge_out[s] = jnp.where(tile == 0, cube[height - 1], cube[0])
    edge_out[2:frames] = edge_in[...]
    copy = pltpu.make_async_copy(result, block_out.at[0:2], leaving)
    copy.start()
    grads = jnp.concatenate(
        [
            part
            for s in range(2)
            for part in [firsts[s][1].T]
            + [turned[p, s * channels : (s + 1) * channels] for p in range(frames // 2 - 1)]
        ],
        axis=1,
    )
    return grads, summed, copy


def leaving_half_kernel(
    block_in, x, before, bias, cotangent, windows, taps, turned, edge_in, total, begun,
    block_out, grad_pre, edge_out, sent, blocks, front, grads, total_out,
    bias_here, upstream, result, arriving, leaving,
):
    tile = lax.axis_index("tile")
    me = lax.axis_index("dp")
    front[2:4] = windows[0:2]
    values, summed, copy = first_frames(
        x, before, bias, cotangent, windows, taps, turned, edge_in, total, begun, block_out, grad_pre, edge_out,
        front, bias_here, upstream, result, arriving, leaving,
    )
    grads[...] = values
    total_out[...] = summed
    group_loop(LEAVING, front, windows, grads, blocks, tile)
    for own in range(2):

        @pl.when(tile == own)
        def _():
            place_half(sent, 1 - own, lambda g, low, high: blocks[g, low:high], summed, me)

    copy.wait()


def staying_half_kernel(blocks_in, front, windows, grads, total, kept, blocks):
    tile = lax.axis_index("tile")
    me = lax.axis_index("dp")
    group_loop(STAYING, front, windows, grads, blocks, tile)
    for own in range(2):
        mine = [STAYING[own] >> 4 * i & 15 for i in range(COUNTS[STAYING][0])]

        @pl.when(tile == own)
        def _():
            place_half(
                kept,
                own,
                lambda g, low, high: (blocks if g in mine else blocks_in)[g, low:high],
                total[...],
                me,
            )


def whole_weights_kernel(
    block_in, x, before, bias, cotangent, windows, taps, turned, edge_in, total, begun,
    block_out, grad_pre, edge_out, weights, bias_sum,
    early, bias_here, upstream, result, arriving, leaving,
):
    frames, height, breadth, channels = x.shape
    grads, summed, copy = first_frames(
        x, before, bias, cotangent, windows, taps, turned, edge_in, total, begun, block_out, grad_pre, edge_out,
        early, bias_here, upstream, result, arriving, leaving,
    )
    for b in range(3):
        for a in range(3):
            source = jnp.concatenate(
                [
                    (early[t + a, b : b + height] if t + a < 2 else windows[t + a - 2, b : b + height])
                    .reshape(-1, 3 * channels)
                    for s in range(2)
                    for t in range(s, frames, 2)
                ],
                axis=0,
            )
            product = jnp.dot(grads, source, preferred_element_type=F32).astype(BF16)
            for e in range(3):
                weights[(a * 3 + b) * 3 + e] = product[:, e * channels : (e + 1) * channels].T
    bias_sum[...] = summed
    copy.wait()


def back_pair(frames, taps, upstream):
    back = lax.dot_general(
        window_block(frames), taps[...], (((1,), (1,)), ((), ())), preferred_element_type=F32
    )
    channels = back.shape[1] // 2
    return [
        (
            upstream[s].astype(F32)
            + back[:, s * channels : (s + 1) * channels].reshape(upstream[s].shape)
        ).astype(BF16)
        for s in range(2)
    ]


def back_interior_kernel(
    early, g, edge, kernel, cotangent, grad_input, last, taps, windows, upstream, result, arriving, leaving
):
    frames, height, breadth, channels = cotangent.shape
    tile = lax.axis_index("tile")
    up_copy = pltpu.make_async_copy(cotangent.at[0 : frames - 2], upstream, arriving)
    up_copy.start()
    for f in range(4):
        for s in range(2):
            a = 2 - f + s
            for b in range(3):
                for e in range(3):
                    lanes = ((f * 3 + b) * 3 + e) * channels
                    where = (slice(s * channels, (s + 1) * channels), slice(lanes, lanes + channels))
                    if 0 <= a < 3:
                        k = ((a * 3 + 2 - b) * 3 + 2 - e) * channels
                        taps[where] = kernel[k : k + channels]
                    else:
                        taps[where] = jnp.zeros((channels, channels), BF16)
    for f in range(2):
        fill_windows(windows, f, early[f], edge[f], tile)

    @pl.loop(2, frames)
    def _(f):
        fill_windows(windows, f, g[f - 2], edge[f], tile)

    last[...] = windows[frames - 2 : frames]
    up_copy.wait()

    def leave(p):
        return pltpu.make_async_copy(
            result.at[pl.ds(2 * p, 2)], grad_input.at[pl.ds(2 * p, 2)], leaving
        )

    @pl.loop(0, frames // 2 - 1)
    def _(p):
        pair = back_pair(
            [windows[2 * p + f] for f in range(4)],
            taps,
            [upstream[2 * p], upstream[2 * p + 1]],
        )
        for s in range(2):
            result[2 * p + s] = pair[s]
        leave(p).start()

    @pl.loop(0, frames // 2 - 1)
    def _(p):
        leave(p).wait()


def back_last_kernel(
    grad_in, last, after, taps, cotangent, grad_input, windows, upstream, result, arriving, leaving
):
    frames, height, breadth, channels = cotangent.shape
    tile = lax.axis_index("tile")
    up_copy = pltpu.make_async_copy(cotangent.at[frames - 2 : frames], upstream, arriving)
    up_copy.start()
    for f in range(2):
        fill_windows(windows, f, after[f * height : (f + 1) * height], after[2 * height + f], tile)
    up_copy.wait()
    pair = back_pair(
        [last[0], last[1], windows[0], windows[1]], taps, [upstream[0], upstream[1]]
    )
    for s in range(2):
        result[s] = pair[s]
    copy = pltpu.make_async_copy(result, grad_input.at[frames - 2 : frames], leaving)
    copy.start()
    copy.wait()


def border_kernel(tail, edge, border):
    count = tail.shape[0]
    border[0:count] = tail[...]
    border[count:] = edge[edge.shape[0] - 2 :]


def closing_kernel(own, other, weight, bias, *, scale, arranged):
    tile = lax.axis_index("tile")
    me = lax.axis_index("dp")
    half, channels = own.shape
    mine, theirs = own[...].astype(F32) * scale, other[...].astype(F32) * scale
    halves = jnp.where(tile == 0, mine, theirs), jnp.where(tile == 0, theirs, mine)
    if arranged:
        per = weight.shape[0] // STEP
        at = (len(HALVES[1][0]) * STEP) % half
        for j in range(len(HALVES[0])):

            @pl.when(me == j)
            def _():
                for h in range(2):
                    for position, step, count in runs_of(HALVES[h][j]):
                        q = (step - j * per) * STEP
                        weight[q : q + count * STEP] = halves[h][
                            position * STEP : (position + count) * STEP
                        ]

    else:
        at = weight.shape[0] - half
        weight[0:half] = halves[0]
        weight[half:] = halves[1][0:at]
    line = halves[1][at : at + 1]
    share = bias.shape[1]
    picked = jnp.zeros((1, share), F32)
    for j in range(channels // share):
        picked = jnp.where(me == j, line[:, j * share : (j + 1) * share], picked)
    bias[...] = picked


def bits_of(count):
    return count.bit_length() - 1


def place_of(me, shard, count, tile):
    apart = me ^ shard
    n = bits_of(count)
    plain = apart * 0
    turned = apart * 0
    for k in range(n):
        bit = (apart >> k) & 1
        plain = plain | (bit << (n - 1 - k))
        turned = turned | (bit << k)
    return jnp.where(tile == 0, plain, turned)


def exchange(block, axis, count, bits):
    route = []
    for i in range(count):
        for c in range(2):
            route.append((i * 2 + c, (i ^ bits[c]) * 2 + c))
    return lax.ppermute(block, (axis, "tile"), route)


def added(a, b):
    return (a.astype(F32) + b.astype(F32)).astype(BF16)


def passed_along(block, axis, distance):
    count = lax.axis_size(axis)
    route = [(i - distance, i) for i in range(count) if 0 <= i - distance < count]
    return lax.ppermute(block, axis, route)


def swapped(block):
    return lax.ppermute(block, "tile", [(0, 1), (1, 0)])


def body(activations, kernel, conv_bias, cotangent):
    clip_count, frames, height, breadth, channels = activations.shape
    x, upstream = activations[0], cotangent[0]
    tile = lax.axis_index("tile")
    shards = lax.axis_size("dp")
    steps = lax.axis_size("tm")
    share = 27 * channels // shards
    half = -(-(share + 1) // 32) * 16
    arranged = shards == 4 and channels == 128

    area = height * breadth
    bias = conv_bias.reshape(1, channels)
    cells = jax.ShapeDtypeStruct(x.shape, BF16)

    def arrays(*shapes, kind=BF16):
        return [jax.ShapeDtypeStruct(shape, kind) for shape in shapes]

    def windows_shape(count):
        return (count, height + 2, breadth, 3 * channels)

    def frames_shape(count):
        return (count, height, breadth, channels)

    def call(kernel_body, name, share, shapes, scratch, far_in, far_out, args, aliases=None):
        here, there = pl.BlockSpec(memory_space=pltpu.VMEM), pl.BlockSpec(memory_space=pltpu.HBM)
        return pl.pallas_call(
            kernel_body,
            out_shape=shapes,
            in_specs=[there if i in far_in else here for i in range(len(args))],
            out_specs=[there if i in far_out else here for i in range(len(shapes))],
            scratch_shapes=scratch,
            input_output_aliases=aliases or {},
            compiler_params=pltpu.CompilerParams(vmem_limit_bytes=32 * 2**20),
            cost_estimate=pl.CostEstimate(
                flops=int(share * 4 * 27 * channels * channels * frames * area),
                bytes_accessed=4 * 2**20,
                transcendentals=0,
            ),
            name=name,
        )(*args)

    dma, vmem = pltpu.SemaphoreType.DMA, pltpu.VMEM
    row = jnp.where(tile == 0, height - 1, 0)
    edge = swapped(lax.dynamic_index_in_dim(x, row, 1, False))
    (border,) = call(
        border_kernel,
        "border_rows",
        2.0,
        arrays((2 * height + 2, breadth, channels)),
        [],
        (),
        (),
        (x[frames - 2 :].reshape(2 * height, breadth, channels), edge),
    )
    before = passed_along(border, "tm", 1)
    block_out, windows, taps, turned, later_grads, later_edge, total, begun = call(
        interior_kernel,
        "forward_interior",
        0.75,
        [cells]
        + arrays(
            windows_shape(frames),
            (36 * channels, 2 * channels),
            (frames // 2 - 1, 2 * channels, area),
            frames_shape(frames - 2),
            (frames - 2, breadth, channels),
        )
        + arrays((1, channels), (area, 2 * channels), kind=F32),
        [
            vmem((1, channels), F32),
            vmem(frames_shape(frames - 2), BF16),
            vmem(frames_shape(frames - 2), BF16),
            dma((2,)),
            dma,
        ],
        (3, 4),
        (0,),
        (x, edge, kernel, bias, upstream),
    )
    front_scratch = [
        vmem((1, channels), F32),
        vmem(frames_shape(2), BF16),
        vmem(frames_shape(2), BF16),
        dma((2,)),
        dma,
    ]
    firsts = [cells] + arrays(frames_shape(2), (frames, breadth, channels))
    operands = (
        block_out, x, before, bias, upstream, windows, taps, turned, later_edge, total, begun,
    )
    if arranged:
        groups = arrays((9, 3 * channels, channels))
        block_out, early_grads, grad_edge, sent, blocks, front, grads, total = call(
            leaving_half_kernel,
            "first_frames_and_leaving_half",
            0.8,
            firsts
            + arrays((shards, half, channels))
            + groups
            + arrays(windows_shape(4), (channels, frames * area))
            + arrays((1, channels), kind=F32),
            front_scratch,
            (0, 3, 4),
            (0,),
            operands,
            {0: 0},
        )
        (kept,) = call(
            staying_half_kernel,
            "staying_half",
            0.45,
            arrays((shards, half, channels)),
            [vmem((9, 3 * channels, channels), BF16)],
            (),
            (),
            (blocks, front, windows, grads, total),
        )
    else:
        block_out, early_grads, grad_edge, weight, line = call(
            whole_weights_kernel,
            "first_frames_and_weights",
            1.25,
            firsts + arrays((27, channels, channels)) + arrays((1, channels), kind=F32),
            [vmem(windows_shape(2), BF16)] + front_scratch,
            (0, 3, 4),
            (0,),
            operands,
            {0: 0},
        )
        weight = weight.reshape(shards, share, channels)
        line = jnp.broadcast_to(line.astype(BF16)[None], (shards, 1, channels))
        pad = jnp.zeros((shards, 2 * half - share - 1, channels), BF16)
        whole = jnp.concatenate([weight, line, pad], axis=1)
        me = lax.axis_index("dp")
        whole = whole.reshape(shards, 2, half, channels)
        kept, sent = (
            jnp.zeros((shards, half, channels), BF16)
            .at[place_of(me, jnp.arange(shards), shards, side)]
            .set(lax.dynamic_index_in_dim(whole, side, 1, False))
            for side in (tile, 1 - tile)
        )

    total = added(kept, swapped(sent))
    edge = swapped(grad_edge)
    edge, total = lax.optimization_barrier((edge, total))
    grad_input, last, taps = call(
        back_interior_kernel,
        "input_gradient_interior",
        0.75,
        [cells] + arrays(windows_shape(2), (2 * channels, 36 * channels)),
        [
            vmem(windows_shape(frames), BF16),
            vmem(frames_shape(frames - 2), BF16),
            vmem(frames_shape(frames - 2), BF16),
            dma,
            dma,
        ],
        (4,),
        (0,),
        (early_grads, later_grads, edge, kernel, upstream),
    )
    first_edge, last = lax.optimization_barrier((edge[:2], last))
    after = passed_along(
        jnp.concatenate(
            [early_grads.reshape(2 * height, breadth, channels), first_edge], axis=0
        ),
        "tm",
        -1,
    )
    if arranged:
        parts = [exchange(total[k], "dp", shards, (k, k)) for k in (2, 3, 1)]
        total = total[0].astype(F32)
        for part in parts:
            total = total + part.astype(F32)
        total = total.astype(BF16)
    else:
        n = bits_of(shards)
        for k in range(n):
            middle = total.shape[0] // 2
            total = added(
                total[:middle], exchange(total[middle:], "dp", shards, (1 << k, 1 << (n - 1 - k)))
            )
        total = total[0]
    total, grad_input = lax.optimization_barrier((total, grad_input))
    (grad_input,) = call(
        back_last_kernel,
        "input_gradient_last",
        0.25,
        [cells],
        [
            vmem(windows_shape(2), BF16),
            vmem(frames_shape(2), BF16),
            vmem(frames_shape(2), BF16),
            dma,
            dma,
        ],
        (0, 4),
        (0,),
        (grad_input, last, after, taps, upstream),
        {0: 0},
    )
    got = {k: exchange(total, "tm", steps, (k, k if k == 3 else 3 - k)) for k in (3, 2, 1)}
    total = (
        (total.astype(F32) + got[1].astype(F32)) + (got[2].astype(F32) + got[3].astype(F32))
    ).astype(BF16)
    total, grad_input = lax.optimization_barrier((total, grad_input))
    other = swapped(total)
    positions = (
        clip_count * frames * height * breadth * shards * steps * lax.axis_size("tile")
    )
    weight, bias_grad = call(
        functools.partial(closing_kernel, scale=1.0 / math.sqrt(positions), arranged=arranged),
        "scaled_weights",
        0.01,
        arrays((share, channels), (1, channels // shards), kind=F32),
        [],
        (),
        (),
        (total, other),
    )
    return block_out[None], grad_input[None], weight, bias_grad.reshape(channels // shards)


def solution(mesh):
    return jax.shard_map(
        body,
        mesh=mesh,
        in_specs=(P("dp", "tm", "tile", None, None), P(), P(), P("dp", "tm", "tile", None, None)),
        out_specs=(
            P("dp", "tm", "tile", None, None),
            P("dp", "tm", "tile", None, None),
            P("dp", None),
            P("dp"),
        ),
        check_vma=False,
    )
```

```python
import functools
import math

import jax
import jax.numpy as jnp
from jax import lax
from jax.experimental import pallas as pl
from jax.experimental.pallas import tpu as pltpu
from jax.sharding import PartitionSpec as P

F32 = jnp.float32
BF16 = jnp.bfloat16


def shifted_columns(cells, breadth):
    count = cells.shape[0]
    wide = cells.astype(F32)
    column = lax.broadcasted_iota(jnp.int32, cells.shape, 0) % breadth
    left = jnp.where(column == 0, 0.0, pltpu.roll(wide, 1, 0))
    right = jnp.where(column == breadth - 1, 0.0, pltpu.roll(wide, count - 1, 0))
    return left.astype(BF16), cells, right.astype(BF16)


def fill_windows(windows, frame, inner, edge, tile):
    height, breadth, channels = inner.shape
    parts = shifted_columns(inner.reshape(height * breadth, channels), breadth)
    edges = shifted_columns(edge, breadth)
    for e in range(3):
        lanes = slice(e * channels, (e + 1) * channels)
        windows[frame, 1 : height + 1, :, lanes] = parts[e].reshape(height, breadth, channels)
        rim = edges[e]
        none = jnp.zeros_like(rim)
        windows[frame, 0, :, lanes] = jnp.where(tile == 0, none, rim)
        windows[frame, height + 1, :, lanes] = jnp.where(tile == 0, rim, none)


def window_block(frames):
    blocks = []
    for frame in frames:
        height = frame.shape[0] - 2
        for b in range(3):
            blocks.append(frame[b : b + height].reshape(-1, frame.shape[-1]))
    return jnp.concatenate(blocks, axis=1)


def activate(pre, source, upstream):
    sigma = jax.nn.sigmoid(pre)
    result = (source.astype(F32) + pre * sigma).astype(BF16)
    grad = (upstream.astype(F32) * sigma * (1.0 + pre * (1.0 - sigma))).astype(BF16)
    return result, grad


def forward_pair(frames, taps, bias, x_pair, upstream, begun=0.0):
    channels = bias.shape[1]
    both = jnp.concatenate([bias[...], bias[...]], axis=1)
    count = 9 * channels * len(frames)
    pre = both + begun + jnp.dot(window_block(frames), taps[0:count], preferred_element_type=F32)
    return [
        activate(
            pre[:, s * channels : (s + 1) * channels],
            x_pair[s].reshape(-1, channels),
            upstream[s].reshape(-1, channels),
        )
        for s in range(2)
    ]


def interior_kernel(
    x,
    edge,
    kernel,
    bias,
    cotangent,
    block_out,
    windows,
    taps,
    turned,
    grad_pre,
    edge_out,
    total,
    begun,
    bias_here,
    upstream,
    result,
    arriving,
    leaving,
):
    frames, height, breadth, channels = x.shape
    area = height * breadth
    tile = lax.axis_index("tile")
    bias_copy = pltpu.make_async_copy(bias, bias_here, arriving.at[0])
    up_copy = pltpu.make_async_copy(cotangent.at[2:frames], upstream, arriving.at[1])
    bias_copy.start()
    up_copy.start()
    rows = 9 * channels
    taps[0 : 3 * rows, 0:channels] = kernel[...]
    taps[3 * rows :, 0:channels] = jnp.zeros((rows, channels), BF16)
    taps[0:rows, channels:] = jnp.zeros((rows, channels), BF16)
    taps[rows:, channels:] = kernel[...]
    @pl.loop(0, frames, unroll=2)
    def _(f):
        fill_windows(windows, f, x[f], edge[f], tile)

    begun[...] = jnp.dot(
        window_block([windows[0], windows[1]]), taps[2 * rows :], preferred_element_type=F32
    )

    bias_copy.wait()
    up_copy.wait()
    total[...] = jnp.zeros((1, channels), F32)

    def leave(p):
        return pltpu.make_async_copy(
            result.at[pl.ds(2 * p, 2)], block_out.at[pl.ds(2 * p + 2, 2)], leaving
        )

    @pl.loop(0, frames // 2 - 1, unroll=True)
    def _(p):
        outs = forward_pair(
            [windows[2 * p + f] for f in range(4)],
            taps,
            bias_here,
            [x[2 * p + 2], x[2 * p + 3]],
            [upstream[2 * p], upstream[2 * p + 1]],
        )
        summed = jnp.zeros((1, channels), F32)
        for s in range(2):
            t = 2 * p + s
            result[t] = outs[s][0].reshape(height, breadth, channels)
            grad = outs[s][1]
            summed = summed + jnp.sum(grad.astype(F32), axis=0, keepdims=True)
            cube = grad.reshape(height, breadth, channels)
            grad_pre[t] = cube
            edge_out[t] = jnp.where(tile == 0, cube[height - 1], cube[0])
        turned[p] = jnp.concatenate([outs[0][1], outs[1][1]], axis=1).T
        total[...] += summed
        leave(p).start()

    @pl.loop(0, frames // 2 - 1)
    def _(p):
        leave(p).wait()


STEP = 32
GROUP = 12
HALVES = (
    (
        (*range(0, 12), 24, 25),
        (*range(36, 48), 27, 28),
        (*range(60, 74),),
        (*range(84, 96), 81, 82),
    ),
    (
        (*range(12, 24), 26),
        (*range(29, 36), *range(48, 54)),
        (*range(54, 60), *range(74, 81)),
        (*range(96, 108), 83),
    ),
)
LEAVING = (0x864210, 0x765320)
STAYING = (0x753, 0x841)
COUNTS = {LEAVING: (6, 3), STAYING: (3, 3)}


def runs_of(steps):
    runs = []
    for position, step in enumerate(steps):
        if runs and step == runs[-1][1] + runs[-1][2] and step % GROUP:
            runs[-1][2] += 1
        else:
            runs.append([position, step, 1])
    return runs


def place_half(target, half, blocks, total, me):
    for j, steps in enumerate(HALVES[half]):
        spot = me ^ j
        for position, step, count in runs_of(steps):
            g, at = step // GROUP, step % GROUP * STEP
            target[spot, position * STEP : (position + count) * STEP] = blocks(
                g, at, at + count * STEP
            )
        if half == 1:
            line = jnp.concatenate(
                [total, jnp.zeros((STEP - 1, total.shape[1]), F32)], axis=0
            ).astype(BF16)
            target[spot, len(steps) * STEP : (len(steps) + 1) * STEP] = line


def group_loop(codes, front, windows, grads, blocks, tile):
    channels = grads.shape[0]
    frames = windows.shape[0]
    height = windows.shape[1] - 2
    code = jnp.where(tile == 0, codes[0], codes[1])
    count, together = COUNTS[codes]

    @pl.loop(0, count // together)
    def _(i):
        for k in range(together):
            g = lax.shift_right_logical(code, 4 * (together * i + k)) & 15
            a, b = g // 3, g % 3
            source = jnp.concatenate(
                [
                    (
                        front[t + a, pl.ds(b, height)]
                        if t < 2
                        else windows[t - 2 + a, pl.ds(b, height)]
                    ).reshape(-1, 3 * channels)
                    for s in range(2)
                    for t in range(s, frames, 2)
                ],
                axis=0,
            )
            product = jnp.dot(grads[...], source, preferred_element_type=F32).astype(BF16)
            for e in range(3):
                lanes = slice(e * channels, (e + 1) * channels)
                blocks[g, lanes] = product[:, lanes].T


def first_frames(
    x, before, bias, cotangent, windows, taps, turned, edge_in, total, begun, block_out, grad_pre, edge_out,
    early, bias_here, upstream, result, arriving, leaving,
):
    frames, height, breadth, channels = x.shape
    tile = lax.axis_index("tile")
    bias_copy = pltpu.make_async_copy(bias, bias_here, arriving.at[0])
    up_copy = pltpu.make_async_copy(cotangent.at[0:2], upstream, arriving.at[1])
    bias_copy.start()
    up_copy.start()
    for f in range(2):
        fill_windows(early, f, before[f * height : (f + 1) * height], before[2 * height + f], tile)
    bias_copy.wait()
    up_copy.wait()
    summed = total[...]
    firsts = forward_pair(
        [early[0], early[1]],
        taps,
        bias_here,
        [x[0], x[1]],
        [upstream[0], upstream[1]],
        begun[...],
    )
    for s in range(2):
        result[s] = firsts[s][0].reshape(height, breadth, channels)
        cube = firsts[s][1].reshape(height, breadth, channels)
        summed = summed + jnp.sum(firsts[s][1].astype(F32), axis=0, keepdims=True)
        grad_pre[s] = cube
        edge_out[s] = jnp.where(tile == 0, cube[height - 1], cube[0])
    edge_out[2:frames] = edge_in[...]
    copy = pltpu.make_async_copy(result, block_out.at[0:2], leaving)
    copy.start()
    grads = jnp.concatenate(
        [
            part
            for s in range(2)
            for part in [firsts[s][1].T]
            + [turned[p, s * channels : (s + 1) * channels] for p in range(frames // 2 - 1)]
        ],
        axis=1,
    )
    return grads, summed, copy


def leaving_half_kernel(
    block_in, x, before, bias, cotangent, windows, taps, turned, edge_in, total, begun,
    block_out, grad_pre, edge_out, sent, blocks, front, grads, total_out,
    bias_here, upstream, result, arriving, leaving,
):
    tile = lax.axis_index("tile")
    me = lax.axis_index("dp")
    front[2:4] = windows[0:2]
    values, summed, copy = first_frames(
        x, before, bias, cotangent, windows, taps, turned, edge_in, total, begun, block_out, grad_pre, edge_out,
        front, bias_here, upstream, result, arriving, leaving,
    )
    grads[...] = values
    total_out[...] = summed
    group_loop(LEAVING, front, windows, grads, blocks, tile)
    for own in range(2):

        @pl.when(tile == own)
        def _():
            place_half(sent, 1 - own, lambda g, low, high: blocks[g, low:high], summed, me)

    copy.wait()


def staying_half_kernel(blocks_in, front, windows, grads, total, kept, blocks):
    tile = lax.axis_index("tile")
    me = lax.axis_index("dp")
    group_loop(STAYING, front, windows, grads, blocks, tile)
    for own in range(2):
        mine = [STAYING[own] >> 4 * i & 15 for i in range(COUNTS[STAYING][0])]

        @pl.when(tile == own)
        def _():
            place_half(
                kept,
                own,
                lambda g, low, high: (blocks if g in mine else blocks_in)[g, low:high],
                total[...],
                me,
            )


def whole_weights_kernel(
    block_in, x, before, bias, cotangent, windows, taps, turned, edge_in, total, begun,
    block_out, grad_pre, edge_out, weights, bias_sum,
    early, bias_here, upstream, result, arriving, leaving,
):
    frames, height, breadth, channels = x.shape
    grads, summed, copy = first_frames(
        x, before, bias, cotangent, windows, taps, turned, edge_in, total, begun, block_out, grad_pre, edge_out,
        early, bias_here, upstream, result, arriving, leaving,
    )
    for b in range(3):
        for a in range(3):
            source = jnp.concatenate(
                [
                    (early[t + a, b : b + height] if t + a < 2 else windows[t + a - 2, b : b + height])
                    .reshape(-1, 3 * channels)
                    for s in range(2)
                    for t in range(s, frames, 2)
                ],
                axis=0,
            )
            product = jnp.dot(grads, source, preferred_element_type=F32).astype(BF16)
            for e in range(3):
                weights[(a * 3 + b) * 3 + e] = product[:, e * channels : (e + 1) * channels].T
    bias_sum[...] = summed
    copy.wait()


def back_pair(frames, taps, upstream):
    back = lax.dot_general(
        window_block(frames), taps[...], (((1,), (1,)), ((), ())), preferred_element_type=F32
    )
    channels = back.shape[1] // 2
    return [
        (
            upstream[s].astype(F32)
            + back[:, s * channels : (s + 1) * channels].reshape(upstream[s].shape)
        ).astype(BF16)
        for s in range(2)
    ]


def back_interior_kernel(
    early, g, edge, kernel, cotangent, grad_input, last, taps, windows, upstream, result, arriving, leaving
):
    frames, height, breadth, channels = cotangent.shape
    tile = lax.axis_index("tile")
    up_copy = pltpu.make_async_copy(cotangent.at[0 : frames - 2], upstream, arriving)
    up_copy.start()
    for f in range(4):
        for s in range(2):
            a = 2 - f + s
            for b in range(3):
                for e in range(3):
                    lanes = ((f * 3 + b) * 3 + e) * channels
                    where = (slice(s * channels, (s + 1) * channels), slice(lanes, lanes + channels))
                    if 0 <= a < 3:
                        k = ((a * 3 + 2 - b) * 3 + 2 - e) * channels
                        taps[where] = kernel[k : k + channels]
                    else:
                        taps[where] = jnp.zeros((channels, channels), BF16)
    for f in range(2):
        fill_windows(windows, f, early[f], edge[f], tile)

    @pl.loop(2, frames)
    def _(f):
        fill_windows(windows, f, g[f - 2], edge[f], tile)

    last[...] = windows[frames - 2 : frames]
    up_copy.wait()

    def leave(p):
        return pltpu.make_async_copy(
            result.at[pl.ds(2 * p, 2)], grad_input.at[pl.ds(2 * p, 2)], leaving
        )

    @pl.loop(0, frames // 2 - 1)
    def _(p):
        pair = back_pair(
            [windows[2 * p + f] for f in range(4)],
            taps,
            [upstream[2 * p], upstream[2 * p + 1]],
        )
        for s in range(2):
            result[2 * p + s] = pair[s]
        leave(p).start()

    @pl.loop(0, frames // 2 - 1)
    def _(p):
        leave(p).wait()


def back_last_kernel(
    grad_in, last, after, taps, cotangent, grad_input, windows, upstream, result, arriving, leaving
):
    frames, height, breadth, channels = cotangent.shape
    tile = lax.axis_index("tile")
    up_copy = pltpu.make_async_copy(cotangent.at[frames - 2 : frames], upstream, arriving)
    up_copy.start()
    for f in range(2):
        fill_windows(windows, f, after[f * height : (f + 1) * height], after[2 * height + f], tile)
    up_copy.wait()
    pair = back_pair(
        [last[0], last[1], windows[0], windows[1]], taps, [upstream[0], upstream[1]]
    )
    for s in range(2):
        result[s] = pair[s]
    copy = pltpu.make_async_copy(result, grad_input.at[frames - 2 : frames], leaving)
    copy.start()
    copy.wait()


def border_kernel(tail, edge, border):
    count = tail.shape[0]
    border[0:count] = tail[...]
    border[count:] = edge[edge.shape[0] - 2 :]


def closing_kernel(own, other, weight, bias, *, scale, arranged):
    tile = lax.axis_index("tile")
    me = lax.axis_index("dp")
    half, channels = own.shape
    mine, theirs = own[...].astype(F32) * scale, other[...].astype(F32) * scale
    halves = jnp.where(tile == 0, mine, theirs), jnp.where(tile == 0, theirs, mine)
    if arranged:
        per = weight.shape[0] // STEP
        at = (len(HALVES[1][0]) * STEP) % half
        for j in range(len(HALVES[0])):

            @pl.when(me == j)
            def _():
                for h in range(2):
                    for position, step, count in runs_of(HALVES[h][j]):
                        q = (step - j * per) * STEP
                        weight[q : q + count * STEP] = halves[h][
                            position * STEP : (position + count) * STEP
                        ]

    else:
        at = weight.shape[0] - half
        weight[0:half] = halves[0]
        weight[half:] = halves[1][0:at]
    line = halves[1][at : at + 1]
    share = bias.shape[1]
    picked = jnp.zeros((1, share), F32)
    for j in range(channels // share):
        picked = jnp.where(me == j, line[:, j * share : (j + 1) * share], picked)
    bias[...] = picked


def bits_of(count):
    return count.bit_length() - 1


def place_of(me, shard, count, tile):
    apart = me ^ shard
    n = bits_of(count)
    plain = apart * 0
    turned = apart * 0
    for k in range(n):
        bit = (apart >> k) & 1
        plain = plain | (bit << (n - 1 - k))
        turned = turned | (bit << k)
    return jnp.where(tile == 0, plain, turned)


def exchange(block, axis, count, bits):
    route = []
    for i in range(count):
        for c in range(2):
            route.append((i * 2 + c, (i ^ bits[c]) * 2 + c))
    return lax.ppermute(block, (axis, "tile"), route)


def added(a, b):
    return (a.astype(F32) + b.astype(F32)).astype(BF16)


def passed_along(block, axis, distance):
    count = lax.axis_size(axis)
    route = [(i - distance, i) for i in range(count) if 0 <= i - distance < count]
    return lax.ppermute(block, axis, route)


def swapped(block):
    return lax.ppermute(block, "tile", [(0, 1), (1, 0)])


def body(activations, kernel, conv_bias, cotangent):
    clip_count, frames, height, breadth, channels = activations.shape
    x, upstream = activations[0], cotangent[0]
    tile = lax.axis_index("tile")
    shards = lax.axis_size("dp")
    steps = lax.axis_size("tm")
    share = 27 * channels // shards
    half = -(-(share + 1) // 32) * 16
    arranged = shards == 4 and channels == 128

    area = height * breadth
    bias = conv_bias.reshape(1, channels)
    cells = jax.ShapeDtypeStruct(x.shape, BF16)

    def arrays(*shapes, kind=BF16):
        return [jax.ShapeDtypeStruct(shape, kind) for shape in shapes]

    def windows_shape(count):
        return (count, height + 2, breadth, 3 * channels)

    def frames_shape(count):
        return (count, height, breadth, channels)

    def call(kernel_body, name, share, shapes, scratch, far_in, far_out, args, aliases=None):
        here, there = pl.BlockSpec(memory_space=pltpu.VMEM), pl.BlockSpec(memory_space=pltpu.HBM)
        return pl.pallas_call(
            kernel_body,
            out_shape=shapes,
            in_specs=[there if i in far_in else here for i in range(len(args))],
            out_specs=[there if i in far_out else here for i in range(len(shapes))],
            scratch_shapes=scratch,
            input_output_aliases=aliases or {},
            compiler_params=pltpu.CompilerParams(vmem_limit_bytes=32 * 2**20),
            cost_estimate=pl.CostEstimate(
                flops=int(share * 4 * 27 * channels * channels * frames * area),
                bytes_accessed=4 * 2**20,
                transcendentals=0,
            ),
            name=name,
        )(*args)

    dma, vmem = pltpu.SemaphoreType.DMA, pltpu.VMEM
    row = jnp.where(tile == 0, height - 1, 0)
    edge = swapped(lax.dynamic_index_in_dim(x, row, 1, False))
    (border,) = call(
        border_kernel,
        "border_rows",
        2.0,
        arrays((2 * height + 2, breadth, channels)),
        [],
        (),
        (),
        (x[frames - 2 :].reshape(2 * height, breadth, channels), edge),
    )
    before = passed_along(border, "tm", 1)
    block_out, windows, taps, turned, later_grads, later_edge, total, begun = call(
        interior_kernel,
        "forward_interior",
        0.75,
        [cells]
        + arrays(
            windows_shape(frames),
            (36 * channels, 2 * channels),
            (frames // 2 - 1, 2 * channels, area),
            frames_shape(frames - 2),
            (frames - 2, breadth, channels),
        )
        + arrays((1, channels), (area, 2 * channels), kind=F32),
        [
            vmem((1, channels), F32),
            vmem(frames_shape(frames - 2), BF16),
            vmem(frames_shape(frames - 2), BF16),
            dma((2,)),
            dma,
        ],
        (3, 4),
        (0,),
        (x, edge, kernel, bias, upstream),
    )
    front_scratch = [
        vmem((1, channels), F32),
        vmem(frames_shape(2), BF16),
        vmem(frames_shape(2), BF16),
        dma((2,)),
        dma,
    ]
    firsts = [cells] + arrays(frames_shape(2), (frames, breadth, channels))
    operands = (
        block_out, x, before, bias, upstream, windows, taps, turned, later_edge, total, begun,
    )
    if arranged:
        groups = arrays((9, 3 * channels, channels))
        block_out, early_grads, grad_edge, sent, blocks, front, grads, total = call(
            leaving_half_kernel,
            "first_frames_and_leaving_half",
            0.8,
            firsts
            + arrays((shards, half, channels))
            + groups
            + arrays(windows_shape(4), (channels, frames * area))
            + arrays((1, channels), kind=F32),
            front_scratch,
            (0, 3, 4),
            (0,),
            operands,
            {0: 0},
        )
        (kept,) = call(
            staying_half_kernel,
            "staying_half",
            0.45,
            arrays((shards, half, channels)),
            [vmem((9, 3 * channels, channels), BF16)],
            (),
            (),
            (blocks, front, windows, grads, total),
        )
    else:
        block_out, early_grads, grad_edge, weight, line = call(
            whole_weights_kernel,
            "first_frames_and_weights",
            1.25,
            firsts + arrays((27, channels, channels)) + arrays((1, channels), kind=F32),
            [vmem(windows_shape(2), BF16)] + front_scratch,
            (0, 3, 4),
            (0,),
            operands,
            {0: 0},
        )
        weight = weight.reshape(shards, share, channels)
        line = jnp.broadcast_to(line.astype(BF16)[None], (shards, 1, channels))
        pad = jnp.zeros((shards, 2 * half - share - 1, channels), BF16)
        whole = jnp.concatenate([weight, line, pad], axis=1)
        me = lax.axis_index("dp")
        whole = whole.reshape(shards, 2, half, channels)
        kept, sent = (
            jnp.zeros((shards, half, channels), BF16)
            .at[place_of(me, jnp.arange(shards), shards, side)]
            .set(lax.dynamic_index_in_dim(whole, side, 1, False))
            for side in (tile, 1 - tile)
        )

    total = added(kept, swapped(sent))
    edge = swapped(grad_edge)
    edge, total = lax.optimization_barrier((edge, total))
    grad_input, last, taps = call(
        back_interior_kernel,
        "input_gradient_interior",
        0.75,
        [cells] + arrays(windows_shape(2), (2 * channels, 36 * channels)),
        [
            vmem(windows_shape(frames), BF16),
            vmem(frames_shape(frames - 2), BF16),
            vmem(frames_shape(frames - 2), BF16),
            dma,
            dma,
        ],
        (4,),
        (0,),
        (early_grads, later_grads, edge, kernel, upstream),
    )
    first_edge, last = lax.optimization_barrier((edge[:2], last))
    after = passed_along(
        jnp.concatenate(
            [early_grads.reshape(2 * height, breadth, channels), first_edge], axis=0
        ),
        "tm",
        -1,
    )
    if arranged:
        parts = [exchange(total[k], "dp", shards, (k, k)) for k in (2, 3, 1)]
        total = total[0].astype(F32)
        for part in parts:
            total = total + part.astype(F32)
        total = total.astype(BF16)
    else:
        n = bits_of(shards)
        for k in range(n):
            middle = total.shape[0] // 2
            total = added(
                total[:middle], exchange(total[middle:], "dp", shards, (1 << k, 1 << (n - 1 - k)))
            )
        total = total[0]
    total, grad_input = lax.optimization_barrier((total, grad_input))
    (grad_input,) = call(
        back_last_kernel,
        "input_gradient_last",
        0.25,
        [cells],
        [
            vmem(windows_shape(2), BF16),
            vmem(frames_shape(2), BF16),
            vmem(frames_shape(2), BF16),
            dma,
            dma,
        ],
        (0, 4),
        (0,),
        (grad_input, last, after, taps, upstream),
        {0: 0},
    )
    got = {k: exchange(total, "tm", steps, (k, k if k == 3 else 3 - k)) for k in (3, 2, 1)}
    total = (
        (total.astype(F32) + got[1].astype(F32)) + (got[2].astype(F32) + got[3].astype(F32))
    ).astype(BF16)
    total, grad_input = lax.optimization_barrier((total, grad_input))
    other = swapped(total)
    positions = (
        clip_count * frames * height * breadth * shards * steps * lax.axis_size("tile")
    )
    weight, bias_grad = call(
        functools.partial(closing_kernel, scale=1.0 / math.sqrt(positions), arranged=arranged),
        "scaled_weights",
        0.01,
        arrays((share, channels), (1, channels // shards), kind=F32),
        [],
        (),
        (),
        (total, other),
    )
    return block_out[None], grad_input[None], weight, bias_grad.reshape(channels // shards)


def solution(mesh):
    return jax.shard_map(
        body,
        mesh=mesh,
        in_specs=(P("dp", "tm", "tile", None, None), P(), P(), P("dp", "tm", "tile", None, None)),
        out_specs=(
            P("dp", "tm", "tile", None, None),
            P("dp", "tm", "tile", None, None),
            P("dp", None),
            P("dp"),
        ),
        check_vma=False,
    )
```
